256 devices in a mesh: occ: 32 (over y_lo, z, core), vir: 8 (over y_hi, x).
Axes of the slice: x: 4, y: 4 (y_hi: 2, y_lo: 2; y = y_hi * 2 + y_lo), z: 8, core: 2. Of those that a mesh axis runs over, the one named last changes fastest.
Arguments:
- three_index: bfloat16 [64, 512, 12288], P('occ', 'vir'), may hold values from -0.059814453 to 0.059814453
- occ_energy: float32 [64], replicated, may hold values from -2 to -0.5
- vir_energy: float32 [512], replicated, may hold values from 0.2 to 3
- partner: int32 [32], P('occ'), may hold values from 0 to 31, as said below
Outputs:
- occ_density: float32 [64, 2], P('occ')
- vir_density: float32 [512, 512], P('vir', 'occ')
The draws below stay inside these ranges and needn't reach their ends.
Inputs may be any that keep to these rules, and one draw needn't show every extreme that they name: partner[p] = p XOR m for one m of 1 to 31 drawn anew in each draw; 32 is a power of two.
All inputs are finite; a program needn't handle non-finite values.
Results may differ from the reference program's by a relative error of at most 0.0009.
Values may be sent and summed in bfloat16 or wider, within the bound.
No kernel may reach another device: no remote copies, remote signals or barrier semaphores. Data moves between devices by JAX's collectives and lax.ppermute only.
A program may use at most 128 MiB of HBM per device.

```python
import jax
import jax.numpy as jnp
from jax import lax

NAUX = 12288
OB = 2
BLOCKS = 32
NOCC = 64
NVIR = 512


def draw_partner(key, part):
    key = jax.random.fold_in(key, 7)
    offset = jax.random.randint(key, (), 1, BLOCKS)
    return jnp.bitwise_xor(jnp.arange(BLOCKS, dtype=jnp.int32), offset).astype(jnp.int32)


def shard_levels(own_key, extent, shards, smallest, largest):
    factor_of, own = 1.0, jax.random.fold_in(own_key, 6)
    for axis_at, blocks in shards:
        steps = jnp.exp(jax.random.uniform(jax.random.fold_in(own, axis_at), (blocks,), jnp.float32, smallest / len(shards), largest / len(shards)))
        factor_of = factor_of * jnp.repeat(steps, extent[axis_at] // blocks).reshape([-1 if axis == axis_at else 1 for axis in range(len(extent))])
    return factor_of


def gaussian(own_key, extent, spread, bound, pieces=(), kind=jnp.bfloat16):
    factor_of = shard_levels(own_key, extent, pieces, -0.22, 0.18) if pieces else 1.0
    entries = jax.random.normal(own_key, extent, jnp.float32) * spread * factor_of
    return jnp.minimum(jnp.maximum(entries, -bound), bound).astype(kind)


def setup_inputs(seed: int = 0) -> dict:
    arg_keys = jax.random.split(jax.random.key(seed), 5)
    three_index = gaussian(arg_keys[0], (NOCC, NVIR, NAUX), 0.01, 0.059814453, ((0, 32), (1, 8)))
    occ_energy = jnp.clip(jax.random.uniform(arg_keys[1], (NOCC,), jnp.float32, -2.0, -0.5), -2.0, -0.5)
    vir_energy = jnp.clip(jax.random.uniform(arg_keys[2], (NVIR,), jnp.float32, 0.2, 3.0), 0.2, 3.0)
    partner = draw_partner(jax.random.fold_in(arg_keys[4], 71), 0)
    return {"three_index": three_index, "occ_energy": occ_energy, "vir_energy": vir_energy, "partner": partner}


def reference(three_index, occ_energy, vir_energy, partner):
    q_rows = three_index.shape[2]

    def one_block(total, block):
        mate = partner[block]
        own = lax.dynamic_slice_in_dim(three_index, (block * OB).astype(jnp.int32), OB, 0)
        other = lax.dynamic_slice_in_dim(three_index, (mate * OB).astype(jnp.int32), OB, 0)
        pair = lax.dot_general(own.reshape(-1, q_rows), other.reshape(-1, q_rows),
                               (((1,), (1,)), ((), ())), preferred_element_type=jnp.float32)
        pair = pair.reshape(OB, NVIR, OB, NVIR)
        e_own = lax.dynamic_slice_in_dim(occ_energy, (block * OB).astype(jnp.int32), OB)
        e_mate = lax.dynamic_slice_in_dim(occ_energy, (mate * OB).astype(jnp.int32), OB)
        denom = (e_own[:, None, None, None] - vir_energy[None, :, None, None]
                 + e_mate[None, None, :, None] - vir_energy[None, None, None, :])
        amps = (pair / denom).astype(jnp.bfloat16)
        swapped = jnp.transpose(pair, (0, 3, 2, 1))
        contra = ((2.0 * pair - swapped) / denom).astype(jnp.bfloat16)
        amps_f = amps.astype(jnp.float32)
        contra_f = contra.astype(jnp.float32)
        occ_part = -jnp.einsum("iajb,kajb->ik", amps_f, contra_f)
        vir_part = jnp.einsum("iajc,ibjc->ab", amps_f, contra_f)
        return total + vir_part, occ_part

    vir_total, occ_rows = lax.scan(one_block, jnp.zeros((NVIR, NVIR), jnp.float32),
                                   jnp.arange(BLOCKS, dtype=jnp.int32))
    return occ_rows.reshape(NOCC, OB), vir_total
```

```python
import functools

import jax
import jax.numpy as jnp
from jax import lax
from jax.experimental import pallas as pl
from jax.experimental.pallas import tpu as pltpu
from jax.sharding import PartitionSpec as P

BF = jnp.bfloat16
F32 = jnp.float32
BOTH = ("occ", "vir")
SMEM = pl.BlockSpec(memory_space=pltpu.SMEM)
VMEM = pl.BlockSpec(memory_space=pltpu.VMEM)
PARAMS = pltpu.CompilerParams(vmem_limit_bytes=48 * 1024 * 1024)


def spread_kernel(x_ref, o_ref, sems):
    parts, q = o_ref.shape[0], o_ref.shape[3]
    copies = [
        pltpu.make_async_copy(x_ref.at[:, :, pl.ds(r * q, q)], o_ref.at[r], sems.at[r])
        for r in range(parts)
    ]
    for c in copies:
        c.start()
    for c in copies:
        c.wait()


def spread(x, parts):
    rows, slab, naux = x.shape
    return pl.pallas_call(
        spread_kernel,
        out_shape=jax.ShapeDtypeStruct((parts, rows, slab, naux // parts), x.dtype),
        in_specs=[pl.BlockSpec(memory_space=pl.ANY)],
        out_specs=pl.BlockSpec(memory_space=pl.ANY),
        scratch_shapes=[pltpu.SemaphoreType.DMA((parts,))],
    )(x)


def product_kernel(a_ref, b_ref, o_ref):
    q = a_ref.shape[-1]
    rows = a_ref[...].reshape(-1, q)
    for k in range(b_ref.shape[1]):
        cols = b_ref[:, k].reshape(-1, q)
        n = cols.shape[0]
        o_ref[:, k * n : (k + 1) * n] = lax.dot_general(
            rows, cols, (((1,), (1,)), ((), ())), preferred_element_type=F32
        ).astype(o_ref.dtype)


def product(got):
    ranks, ob, slab, q = got.shape
    nv = ranks // 2
    n = nv * ob * slab
    step = 2
    return pl.pallas_call(
        product_kernel,
        grid=(nv // step,),
        out_shape=jax.ShapeDtypeStruct((n, n), BF),
        in_specs=[
            pl.BlockSpec((step, ob, slab, q), lambda r: (r, 0, 0, 0)),
            pl.BlockSpec((nv, ob, slab, q), lambda r: (1, 0, 0, 0)),
        ],
        out_specs=pl.BlockSpec((step * ob * slab, n), lambda r: (r, 0)),
        compiler_params=PARAMS,
    )(got, got)


def gather_sum_kernel(side_ref, p_ref, keep_ref, send_ref, turn_ref):
    total = p_ref[0].astype(F32)
    for src in range(1, p_ref.shape[0]):
        total += p_ref[src].astype(F32)
    ob, half = keep_ref.shape[:2]
    first = side_ref[0] == 0
    for i in range(ob):
        low = total[2 * half * i : 2 * half * i + half]
        high = total[2 * half * i + half : 2 * half * (i + 1)]
        keep_ref[i] = jnp.where(first, low, high)
        send_ref[i] = jnp.where(first, high, low).astype(BF)
    turned = total.T
    for w in range(2):
        for s in range(2):
            at = (2 * w + s) * half
            turn_ref[s, w, 0] = turned[at : at + half].astype(BF)


def gather_sum(side, parts, ob, slab):
    nv, rows, cols = parts.shape
    half = slab // 2
    per_k = cols // ob // (2 * slab)
    return pl.pallas_call(
        gather_sum_kernel,
        grid=(cols // (2 * slab),),
        out_shape=[
            jax.ShapeDtypeStruct((ob, half, cols), F32),
            jax.ShapeDtypeStruct((ob, half, cols), BF),
            jax.ShapeDtypeStruct((2, nv, ob, half, rows), BF),
        ],
        in_specs=[SMEM, pl.BlockSpec((nv, rows, 2 * slab), lambda j: (0, 0, j))],
        out_specs=[
            pl.BlockSpec((ob, half, 2 * slab), lambda j: (0, 0, j)),
            pl.BlockSpec((ob, half, 2 * slab), lambda j: (0, 0, j)),
            pl.BlockSpec((2, 2, 1, half, rows), lambda j: (0, j % per_k, j // per_k, 0, 0)),
        ],
        compiler_params=PARAMS,
    )(side, parts)


def density_kernel(e_ref, keep_ref, come_ref, turn_ref, vc_ref, vall_ref, o_ref):
    ob, half, cols = keep_ref.shape
    nvir = cols // ob
    nv = turn_ref.shape[1]
    lanes = turn_ref.shape[-1]
    low = lax.broadcasted_iota(jnp.int32, (half, lanes), 1) < lanes // 2

    def swap(x):
        return pltpu.roll(x, lanes // 2, 1)

    turned = [[None] * ob for _ in range(ob)]
    for k in range(ob):
        cs = [turn_ref[0, w, k].astype(F32) + turn_ref[1, w, k].astype(F32) for w in range(nv)]
        pairs = [(cs[w], cs[w + 1]) for w in range(0, nv, 2)]
        turned[0][k] = jnp.concatenate([jnp.where(low, x, swap(y)) for x, y in pairs], axis=1)
        turned[1][k] = jnp.concatenate([jnp.where(low, swap(x), y) for x, y in pairs], axis=1)
    t1, c1, t2, c2 = {}, {}, {}, {}
    for i in range(ob):
        for k in range(ob):
            cut = slice(k * nvir, (k + 1) * nvir)
            x1 = keep_ref[i, :, cut] + come_ref[i, :, cut].astype(F32)
            x2 = turned[i][k]
            denom = (e_ref[i] + e_ref[ob + k]) - vc_ref[...] - vall_ref[...]
            t1[i, k] = (x1 / denom).astype(BF)
            t2[i, k] = (x2 / denom).astype(BF)
            c1[i, k] = ((2.0 * x1 - x2) / denom).astype(BF)
            c2[i, k] = ((2.0 * x2 - x1) / denom).astype(BF)
    order = [(i, k) for i in range(ob) for k in range(ob)]
    amps = jnp.concatenate([t1[x] for x in order] + [t2[x] for x in order], axis=0)
    contra = jnp.concatenate([c1[x] for x in order] + [c2[x] for x in order], axis=0)
    vt = lax.dot_general(contra, amps, (((0,), (0,)), ((), ())), preferred_element_type=F32)
    split = vt.reshape(nvir // 16, 2, 8, nvir)
    h0 = split[:, 0].reshape(nvir // 2, nvir)
    h1 = split[:, 1].reshape(nvir // 2, nvir)
    low = lax.broadcasted_iota(jnp.int32, (nvir // 2, lanes), 1) < lanes // 2
    for j in range(nv // 2):
        x, y = h0[:, j * lanes : (j + 1) * lanes], h1[:, j * lanes : (j + 1) * lanes]
        o_ref[2 * j, : nvir // 2] = jnp.where(low, x, swap(y)).astype(o_ref.dtype)
        o_ref[2 * j + 1, : nvir // 2] = jnp.where(low, swap(x), y).astype(o_ref.dtype)

    def dot(x, y):
        rows = jnp.sum(x.astype(F32) * y.astype(F32), axis=0, keepdims=True)
        return sum(rows[:, j * lanes : (j + 1) * lanes] for j in range(nvir // lanes))

    occ = [-sum(dot(t1[i, k], c1[m, k]) for k in range(ob)) for i in range(ob) for m in range(ob)]
    occ += [-sum(dot(t2[i, k], c2[i, n]) for i in range(ob)) for k in range(ob) for n in range(ob)]
    occ = jnp.concatenate(occ, axis=0)
    high = occ.astype(BF)
    rest = (occ - high.astype(F32)).astype(BF)
    tail = jnp.concatenate([high, rest], axis=0).astype(o_ref.dtype)
    for v in range(nv):
        o_ref[v, nvir // 2 :] = tail


def density(energies, keep, come, turned, vc, vall, slab):
    nv = turned.shape[1]
    nvir = vall.shape[1]
    return pl.pallas_call(
        density_kernel,
        out_shape=jax.ShapeDtypeStruct((nv, nvir // 2 + 16, 2 * slab), BF),
        in_specs=[SMEM] + [VMEM] * 5,
        out_specs=VMEM,
        compiler_params=PARAMS,
    )(energies, keep, come, turned, vc, vall)


def lane_sum_kernel(at_ref, p_ref, o_ref):
    total = p_ref[0].astype(F32)
    for src in range(1, p_ref.shape[0]):
        total += p_ref[src].astype(F32)
    count = o_ref.shape[0]
    n = 8 * count
    occ = total[n : n + 8] + total[n + 8 : n + 16]
    other = pltpu.roll(occ, 4, 0)
    first = at_ref[0] < at_ref[1]
    mine = jnp.where(first, occ, other)
    theirs = jnp.where(first, other, occ)
    for o in range(count):
        o_ref[o, :8] = total[8 * o : 8 * o + 8]
        o_ref[o, 8:] = jnp.where(at_ref[0] == o, mine, jnp.where(at_ref[1] == o, theirs, 0.0))


def lane_sum(at, parts, count):
    return pl.pallas_call(
        lane_sum_kernel,
        out_shape=jax.ShapeDtypeStruct((count, 16, parts.shape[2]), F32),
        in_specs=[SMEM, VMEM],
        out_specs=VMEM,
        compiler_params=PARAMS,
    )(at, parts)


def last_sum_kernel(p_ref, occ_ref, vir_ref):
    total = p_ref[0]
    for src in range(1, p_ref.shape[0]):
        total += p_ref[src]
    turned = total[:8].T
    slab = turned.shape[0] // 2
    vir_ref[:, :8] = turned[:slab]
    vir_ref[:, 8:] = turned[slab:]
    occ = jnp.sum(total[8:], axis=1, keepdims=True)
    ob = occ_ref.shape[0]
    for i in range(ob):
        for m in range(ob):
            occ_ref[i : i + 1, m : m + 1] = occ[ob * i + m : ob * i + m + 1]


def last_sum(parts, ob, slab):
    return pl.pallas_call(
        last_sum_kernel,
        out_shape=[
            jax.ShapeDtypeStruct((ob, ob), F32),
            jax.ShapeDtypeStruct((slab, 16), F32),
        ],
        in_specs=[VMEM],
        out_specs=[VMEM, VMEM],
        compiler_params=PARAMS,
    )(parts)


def pair_groups(count, lanes, offset):
    return [
        [p * lanes + v for p in (low, low ^ offset) for v in range(lanes)]
        for low in range(count)
        if low < low ^ offset
    ]


def by_offset(offset, count, branch, *operands):
    branches = [functools.partial(branch, m) for m in range(1, count)]
    return lax.switch(offset - 1, branches, *operands)


def per_device(three_index, occ_energy, vir_energy, partner):
    ob, slab, naux = three_index.shape
    nvir = vir_energy.shape[0]
    count, lanes = lax.axis_size("occ"), lax.axis_size("vir")
    p, v = lax.axis_index("occ"), lax.axis_index("vir")
    q = partner[0]
    offset = jnp.bitwise_xor(p, q)
    side = (p > q).astype(jnp.int32)
    low, high = jnp.minimum(p, q), jnp.maximum(p, q)
    half = slab // 2

    def share(m, x):
        return lax.all_to_all(
            x, BOTH, 0, 0, axis_index_groups=pair_groups(count, lanes, m), tiled=True
        )

    chunks = spread(three_index, 2 * lanes)
    got = by_offset(offset, count, share, chunks)
    pair = product(got)
    parts = lax.all_to_all(pair.reshape(lanes, ob * slab, -1), "vir", 0, 0, tiled=True)
    keep, send, turn = gather_sum(side.reshape(1), parts, ob, slab)

    def finish(m, send, turn):
        come = lax.ppermute(send, "occ", [(a, a ^ m) for a in range(count)])
        return come, share(m, turn)

    come, turned = by_offset(
        offset, count, finish, send, turn.reshape(2 * lanes, ob, half, ob * slab)
    )
    energies = jnp.concatenate([
        lax.dynamic_slice_in_dim(occ_energy, low * ob, ob),
        lax.dynamic_slice_in_dim(occ_energy, high * ob, ob),
    ])
    vc = lax.dynamic_slice_in_dim(vir_energy, v * slab + side * half, half)
    packed = density(
        energies, keep, come, turned.reshape(2, lanes, ob, half, ob * slab),
        vc.reshape(half, 1), vir_energy.reshape(1, nvir), slab,
    )
    parts = lax.all_to_all(packed, "vir", 0, 0, tiled=True)
    pieces = lane_sum(jnp.stack([p, q]), parts, count)
    parts = lax.all_to_all(pieces, "occ", 0, 0, tiled=True)
    return tuple(last_sum(parts, ob, slab))


def solution(mesh):
    in_specs = (P("occ", "vir", None), P(), P(), P("occ"))
    out_specs = (P("occ", None), P("vir", "occ"))
    return jax.shard_map(
        per_device, mesh=mesh, in_specs=in_specs, out_specs=out_specs, check_vma=False
    )
```

```python
import functools

import jax
import jax.numpy as jnp
from jax import lax
from jax.experimental import pallas as pl
from jax.experimental.pallas import tpu as pltpu
from jax.sharding import PartitionSpec as P

BF = jnp.bfloat16
F32 = jnp.float32
BOTH = ("occ", "vir")
SMEM = pl.BlockSpec(memory_space=pltpu.SMEM)
VMEM = pl.BlockSpec(memory_space=pltpu.VMEM)
PARAMS = pltpu.CompilerParams(vmem_limit_bytes=48 * 1024 * 1024)


def cut_kernel(side_ref, x_ref, o_ref, sems):
    parts, pieces, _, q = o_ref.shape
    side = side_ref[0]
    copies = []
    for r in range(parts):
        for n in range(pieces):
            half, orbital = (1 - side, 0) if pieces == 1 else ((side, n) if n < 2 else (1 - side, n - 1))
            at = pl.multiple_of((half * parts + r) * q, q)
            copies.append(
                pltpu.make_async_copy(
                    x_ref.at[orbital, :, pl.ds(at, q)], o_ref.at[r, n], sems.at[r, n]
                )
            )
    for c in copies:
        c.start()
    for c in copies:
        c.wait()


def cut(side, x, parts, pieces):
    _, slab, naux = x.shape
    return pl.pallas_call(
        cut_kernel,
        out_shape=jax.ShapeDtypeStruct((parts, pieces, slab, naux // (2 * parts)), x.dtype),
        in_specs=[SMEM, pl.BlockSpec(memory_space=pl.ANY)],
        out_specs=pl.BlockSpec(memory_space=pl.ANY),
        scratch_shapes=[pltpu.SemaphoreType.DMA((parts, pieces))],
    )(side, x)


def product_kernel(side_ref, mine_ref, come_ref, o_ref):
    nv, slab, q = come_ref.shape
    n = nv * slab

    def fill(turn):
        come = come_ref[...].reshape(n, q)
        for j in range(mine_ref.shape[1]):
            mine = mine_ref[:, j].reshape(n, q)
            rows, cols = (come, mine) if turn else (mine, come)
            out = lax.dot_general(rows, cols, (((1,), (1,)), ((), ())), preferred_element_type=F32)
            o_ref[:, :, j * n : (j + 1) * n] = out.astype(BF).reshape(nv, slab, n)

    pl.when(side_ref[0] == 0)(lambda: fill(False))
    pl.when(side_ref[0] != 0)(lambda: fill(True))


def product(side, mine, come, ob):
    nv, slab, q = come.shape
    return pl.pallas_call(
        product_kernel,
        grid=(1,),
        out_shape=jax.ShapeDtypeStruct((nv, slab, ob * nv * slab), BF),
        in_specs=[
            SMEM,
            pl.BlockSpec((nv, ob, slab, q), lambda r: (0, 0, 0, 0)),
            pl.BlockSpec((nv, slab, q), lambda r: (0, 0, 0)),
        ],
        out_specs=pl.BlockSpec((nv, slab, ob * nv * slab), lambda r: (0, 0, 0)),
        compiler_params=PARAMS,
    )(side, mine, come)


def gather_sum_kernel(side_ref, z00_ref, z01_ref, z10_ref, z11_ref, keep_ref, send_ref, turn_ref):
    def sums(ref):
        total = ref[0].astype(F32)
        for src in range(1, ref.shape[0]):
            total += ref[src].astype(F32)
        return total

    first = side_ref[0] == 0
    z00, z01, z10, z11 = sums(z00_ref), sums(z01_ref), sums(z10_ref), sums(z11_ref)
    rows = [[z00, jnp.where(first, z10, z01)], [jnp.where(first, z01, z10), z11]]
    half = keep_ref.shape[2]
    for k in range(2):
        for i in range(2):
            low, high = rows[i][k][:half], rows[i][k][half:]
            keep_ref[i, k] = jnp.where(first, low, high)
            send_ref[i, k] = jnp.where(first, high, low).astype(BF)
        turned = jnp.concatenate([rows[0][k], rows[1][k]], axis=0).T
        for w in range(2):
            for s in range(2):
                at = (2 * w + s) * half
                turn_ref[s, w, k] = turned[at : at + half].astype(BF)


def gather_sum(side, z0, z1):
    nv, slab, cols = z0.shape
    half, nvir = slab // 2, nv * slab
    steps = nvir // (2 * slab)
    low = pl.BlockSpec((nv, slab, 2 * slab), lambda j: (0, 0, j))
    high = pl.BlockSpec((nv, slab, 2 * slab), lambda j: (0, 0, j + steps))
    rows = pl.BlockSpec((2, 2, half, 2 * slab), lambda j: (0, 0, 0, j))
    return pl.pallas_call(
        gather_sum_kernel,
        grid=(steps,),
        out_shape=[
            jax.ShapeDtypeStruct((2, 2, half, nvir), F32),
            jax.ShapeDtypeStruct((2, 2, half, nvir), BF),
            jax.ShapeDtypeStruct((2, nv, 2, half, 2 * slab), BF),
        ],
        in_specs=[SMEM, low, high, low, high],
        out_specs=[
            rows,
            rows,
            pl.BlockSpec((2, 2, 2, half, 2 * slab), lambda j: (0, j, 0, 0, 0)),
        ],
        compiler_params=PARAMS,
    )(side, z0, z0, z1, z1)


def density_kernel(e_ref, keep_ref, come_ref, turn_ref, vc_ref, vall_ref, o_ref):
    ob, _, half, nvir = keep_ref.shape
    nv = turn_ref.shape[1]
    lanes = turn_ref.shape[-1]
    low = lax.broadcasted_iota(jnp.int32, (half, lanes), 1) < lanes // 2

    def swap(x):
        return pltpu.roll(x, lanes // 2, 1)

    turned = [[None] * ob for _ in range(ob)]
    for k in range(ob):
        cs = [turn_ref[0, w, k].astype(F32) + turn_ref[1, w, k].astype(F32) for w in range(nv)]
        pairs = [(cs[w], cs[w + 1]) for w in range(0, nv, 2)]
        turned[0][k] = jnp.concatenate([jnp.where(low, x, swap(y)) for x, y in pairs], axis=1)
        turned[1][k] = jnp.concatenate([jnp.where(low, swap(x), y) for x, y in pairs], axis=1)
    t1, c1, t2, c2 = {}, {}, {}, {}
    for i in range(ob):
        for k in range(ob):
            x1 = keep_ref[i, k] + come_ref[i, k].astype(F32)
            x2 = turned[i][k]
            denom = (e_ref[i] + e_ref[ob + k]) - vc_ref[...] - vall_ref[...]
            t1[i, k] = (x1 / denom).astype(BF)
            t2[i, k] = (x2 / denom).astype(BF)
            c1[i, k] = ((2.0 * x1 - x2) / denom).astype(BF)
            c2[i, k] = ((2.0 * x2 - x1) / denom).astype(BF)
    order = [(i, k) for i in range(ob) for k in range(ob)]
    amps = jnp.concatenate([t1[x] for x in order] + [t2[x] for x in order], axis=0)
    contra = jnp.concatenate([c1[x] for x in order] + [c2[x] for x in order], axis=0)
    vt = lax.dot_general(contra, amps, (((0,), (0,)), ((), ())), preferred_element_type=F32)
    split = vt.reshape(nvir // 16, 2, 8, nvir)
    h0 = split[:, 0].reshape(nvir // 2, nvir)
    h1 = split[:, 1].reshape(nvir // 2, nvir)
    low = lax.broadcasted_iota(jnp.int32, (nvir // 2, lanes), 1) < lanes // 2
    for j in range(nv // 2):
        x, y = h0[:, j * lanes : (j + 1) * lanes], h1[:, j * lanes : (j + 1) * lanes]
        o_ref[2 * j, : nvir // 2] = jnp.where(low, x, swap(y)).astype(o_ref.dtype)
        o_ref[2 * j + 1, : nvir // 2] = jnp.where(low, swap(x), y).astype(o_ref.dtype)

    def dot(x, y):
        rows = jnp.sum(x.astype(F32) * y.astype(F32), axis=0, keepdims=True)
        return sum(rows[:, j * lanes : (j + 1) * lanes] for j in range(nvir // lanes))

    occ = [-sum(dot(t1[i, k], c1[m, k]) for k in range(ob)) for i in range(ob) for m in range(ob)]
    occ += [-sum(dot(t2[i, k], c2[i, n]) for i in range(ob)) for k in range(ob) for n in range(ob)]
    occ = jnp.concatenate(occ, axis=0)
    high = occ.astype(BF)
    rest = (occ - high.astype(F32)).astype(BF)
    tail = jnp.concatenate([high, rest], axis=0).astype(o_ref.dtype)
    for v in range(nv):
        o_ref[v, nvir // 2 :] = tail


def density(energies, keep, come, turned, vc, vall, slab):
    nv = turned.shape[1]
    nvir = vall.shape[1]
    return pl.pallas_call(
        density_kernel,
        out_shape=jax.ShapeDtypeStruct((nv, nvir // 2 + 16, 2 * slab), BF),
        in_specs=[SMEM] + [VMEM] * 5,
        out_specs=VMEM,
        compiler_params=PARAMS,
    )(energies, keep, come, turned, vc, vall)


def lane_sum_kernel(at_ref, p_ref, o_ref):
    total = p_ref[0].astype(F32)
    for src in range(1, p_ref.shape[0]):
        total += p_ref[src].astype(F32)
    count = o_ref.shape[0]
    n = 8 * count
    occ = total[n : n + 8] + total[n + 8 : n + 16]
    other = pltpu.roll(occ, 4, 0)
    first = at_ref[0] < at_ref[1]
    mine = jnp.where(first, occ, other)
    theirs = jnp.where(first, other, occ)
    for o in range(count):
        o_ref[o, :8] = total[8 * o : 8 * o + 8]
        o_ref[o, 8:] = jnp.where(at_ref[0] == o, mine, jnp.where(at_ref[1] == o, theirs, 0.0))


def lane_sum(at, parts, count):
    return pl.pallas_call(
        lane_sum_kernel,
        out_shape=jax.ShapeDtypeStruct((count, 16, parts.shape[2]), F32),
        in_specs=[SMEM, VMEM],
        out_specs=VMEM,
        compiler_params=PARAMS,
    )(at, parts)


def last_sum_kernel(p_ref, occ_ref, vir_ref):
    total = p_ref[0]
    for src in range(1, p_ref.shape[0]):
        total += p_ref[src]
    turned = total[:8].T
    slab = turned.shape[0] // 2
    vir_ref[:, :8] = turned[:slab]
    vir_ref[:, 8:] = turned[slab:]
    occ = jnp.sum(total[8:], axis=1, keepdims=True)
    ob = occ_ref.shape[0]
    for i in range(ob):
        for m in range(ob):
            occ_ref[i : i + 1, m : m + 1] = occ[ob * i + m : ob * i + m + 1]


def last_sum(parts, ob, slab):
    return pl.pallas_call(
        last_sum_kernel,
        out_shape=[
            jax.ShapeDtypeStruct((ob, ob), F32),
            jax.ShapeDtypeStruct((slab, 16), F32),
        ],
        in_specs=[VMEM],
        out_specs=[VMEM, VMEM],
        compiler_params=PARAMS,
    )(parts)


def pair_groups(count, lanes, offset):
    return [
        [p * lanes + v for p in (low, low ^ offset) for v in range(lanes)]
        for low in range(count)
        if low < low ^ offset
    ]


def by_offset(offset, count, branch, *operands):
    branches = [functools.partial(branch, m) for m in range(1, count)]
    return lax.switch(offset - 1, branches, *operands)


def per_device(three_index, occ_energy, vir_energy, partner):
    ob, slab, naux = three_index.shape
    nvir = vir_energy.shape[0]
    count, lanes = lax.axis_size("occ"), lax.axis_size("vir")
    p, v = lax.axis_index("occ"), lax.axis_index("vir")
    q = partner[0]
    offset = jnp.bitwise_xor(p, q)
    side = (p > q).astype(jnp.int32)
    low, high = jnp.minimum(p, q), jnp.maximum(p, q)
    half = slab // 2

    here = side.reshape(1)

    def over_vir(x):
        return lax.all_to_all(x, "vir", 0, 0, tiled=True)

    def exchange(m, x):
        def to_partner(y):
            return lax.ppermute(y, "occ", [(a, a ^ m) for a in range(count)])

        come = to_partner(cut(here, x, lanes, 1)[:, 0])
        mine = over_vir(cut(here, x, lanes, 3))
        later = to_partner(mine[:, 2])
        first = over_vir(product(here, mine, over_vir(come), ob))
        second = over_vir(product(here, mine, later, ob))
        keep, send, turn = gather_sum(here, first, second)
        turned = lax.all_to_all(
            turn.reshape(2 * lanes, ob, half, ob * slab), BOTH, 0, 0,
            axis_index_groups=pair_groups(count, lanes, m), tiled=True,
        )
        return keep, to_partner(send), turned

    keep, come, turned = by_offset(offset, count, exchange, three_index)
    energies = jnp.concatenate([
        lax.dynamic_slice_in_dim(occ_energy, low * ob, ob),
        lax.dynamic_slice_in_dim(occ_energy, high * ob, ob),
    ])
    vc = lax.dynamic_slice_in_dim(vir_energy, v * slab + side * half, half)
    packed = density(
        energies, keep, come, turned.reshape(2, lanes, ob, half, ob * slab),
        vc.reshape(half, 1), vir_energy.reshape(1, nvir), slab,
    )
    parts = lax.all_to_all(packed, "vir", 0, 0, tiled=True)
    pieces = lane_sum(jnp.stack([p, q]), parts, count)
    parts = lax.all_to_all(pieces, "occ", 0, 0, tiled=True)
    return tuple(last_sum(parts, ob, slab))


def solution(mesh):
    in_specs = (P("occ", "vir", None), P(), P(), P("occ"))
    out_specs = (P("occ", None), P("vir", "occ"))
    return jax.shard_map(
        per_device, mesh=mesh, in_specs=in_specs, out_specs=out_specs, check_vma=False
    )
```

```python
import functools

import jax
import jax.numpy as jnp
from jax import lax
from jax.experimental import pallas as pl
from jax.experimental.pallas import tpu as pltpu
from jax.sharding import PartitionSpec as P

BF = jnp.bfloat16
F32 = jnp.float32
BOTH = ("occ", "vir")
SMEM = pl.BlockSpec(memory_space=pltpu.SMEM)
VMEM = pl.BlockSpec(memory_space=pltpu.VMEM)
ANY = pl.BlockSpec(memory_space=pl.ANY)
PARAMS = pltpu.CompilerParams(vmem_limit_bytes=48 * 1024 * 1024)


def cut_kernel(at_ref, x_ref, o_ref, sems):
    parts, _, _, q = o_ref.shape
    copies = []
    for w in range(parts):
        start = pl.multiple_of(((1 - at_ref[0]) * parts + w) * q, q)
        copies.append(
            pltpu.make_async_copy(x_ref.at[:, :, pl.ds(start, q)], o_ref.at[w], sems.at[w])
        )
    for c in copies:
        c.start()
    for c in copies:
        c.wait()


def cut(at, x, parts):
    ob, slab, naux = x.shape
    return pl.pallas_call(
        cut_kernel,
        out_shape=jax.ShapeDtypeStruct((parts, ob, slab, naux // (2 * parts)), x.dtype),
        in_specs=[SMEM, ANY],
        out_specs=VMEM,
        scratch_shapes=[pltpu.SemaphoreType.DMA((parts,))],
        compiler_params=PARAMS,
    )(at, x)


def pick_kernel(at_ref, x_ref, other_ref, lead_ref, rest_ref, sems):
    parts, _, q = lead_ref.shape

    def fill(stays):
        copies = []
        for w in range(parts):
            start = pl.multiple_of((at_ref[0] * parts + w) * q, q)
            own = lambda n: x_ref.at[n, :, pl.ds(start, q)]
            other = lambda n: other_ref.at[w, n]
            stay, leave = (own, other) if stays else (other, own)
            for n, (src, dst) in enumerate([
                (leave(0), lead_ref.at[w]),
                (stay(0), rest_ref.at[w, 0]),
                (stay(1), rest_ref.at[w, 1]),
                (leave(1), rest_ref.at[w, 2]),
            ]):
                copies.append(pltpu.make_async_copy(src, dst, sems.at[w, n]))
        for c in copies:
            c.start()
        for c in copies:
            c.wait()

    pl.when(at_ref[1] != 0)(lambda: fill(True))
    pl.when(at_ref[1] == 0)(lambda: fill(False))


def pick(at, x, other):
    parts, _, slab, q = other.shape
    return pl.pallas_call(
        pick_kernel,
        out_shape=[
            jax.ShapeDtypeStruct((parts, slab, q), x.dtype),
            jax.ShapeDtypeStruct((parts, 3, slab, q), x.dtype),
        ],
        in_specs=[SMEM, ANY, ANY],
        out_specs=[VMEM, VMEM],
        scratch_shapes=[pltpu.SemaphoreType.DMA((parts, 4))],
        compiler_params=PARAMS,
    )(at, x, other)


def product_kernel(mine_ref, come0_ref, come1_ref, o_ref):
    nv, ob, slab, q = mine_ref.shape
    n = nv * slab
    ranks, _, half, _ = o_ref.shape
    for k, come_ref in enumerate((come0_ref, come1_ref)):
        cols = come_ref[...].reshape(n, q)
        for i in range(ob):
            rows = mine_ref[:, i].reshape(n, q)
            out = lax.dot_general(rows, cols, (((1,), (1,)), ((), ())), preferred_element_type=F32)
            o_ref[:, i, :, k * n : (k + 1) * n] = out.astype(BF).reshape(ranks, half, n)


def product(mine, come0, come1, ob):
    nv, slab, q = come0.shape
    shape = (2 * nv, ob, slab // 2, ob * nv * slab)
    come = pl.BlockSpec((nv, slab, q), lambda r: (0, 0, 0))
    return pl.pallas_call(
        product_kernel,
        grid=(1,),
        out_shape=jax.ShapeDtypeStruct(shape, BF),
        in_specs=[pl.BlockSpec((nv, ob, slab, q), lambda r: (0, 0, 0, 0)), come, come],
        out_specs=pl.BlockSpec(shape, lambda r: (0, 0, 0, 0)),
        compiler_params=PARAMS,
    )(mine, come0, come1)


def gather_sum_kernel(p0_ref, p1_ref, keep_ref, turn_ref):
    rows = []
    for k, ref in enumerate((p0_ref, p1_ref)):
        total = ref[0].astype(F32)
        for src in range(1, ref.shape[0]):
            total += ref[src].astype(F32)
        keep_ref[:, k] = total
        rows.append(total.reshape(-1, total.shape[2]))
    turned = jnp.concatenate(rows, axis=0).T
    turn_ref[...] = turned.reshape(turn_ref.shape).astype(BF)


def gather_sum(parts):
    ranks, ob, half, cols = parts.shape
    nvir, lanes = cols // ob, 2 * ob * half
    steps = nvir // lanes
    return pl.pallas_call(
        gather_sum_kernel,
        grid=(steps,),
        out_shape=[
            jax.ShapeDtypeStruct((ob, ob, half, nvir), F32),
            jax.ShapeDtypeStruct((ranks, half, lanes), BF),
        ],
        in_specs=[
            pl.BlockSpec((ranks, ob, half, lanes), lambda j: (0, 0, 0, j)),
            pl.BlockSpec((ranks, ob, half, lanes), lambda j: (0, 0, 0, j + steps)),
        ],
        out_specs=[
            pl.BlockSpec((ob, ob, half, lanes), lambda j: (0, 0, 0, j)),
            pl.BlockSpec((lanes // half, half, lanes), lambda j: (j, 0, 0)),
        ],
        compiler_params=PARAMS,
    )(parts, parts)


def density_kernel(e_ref, keep_ref, turn_ref, vc_ref, vall_ref, o_ref):
    ob, _, half, nvir = keep_ref.shape
    ranks, _, lanes = turn_ref.shape
    nv = ranks // 2
    spots = lanes // half
    spot = lax.broadcasted_iota(jnp.int32, (half, lanes), 1) // half
    turned = {}
    for g in range(ranks // spots):
        moved = []
        for j in range(spots):
            x = turn_ref[g * spots + j].astype(F32)
            moved.append([x] + [pltpu.roll(x, n * half, 1) for n in range(1, spots)])
        for ki in range(spots):
            whole = moved[0][(-ki) % spots]
            for j in range(1, spots):
                whole = jnp.where(spot == j, moved[j][(j - ki) % spots], whole)
            turned.setdefault((ki % ob, ki // ob), []).append(whole)
    turned = {ik: jnp.concatenate(x, axis=1) for ik, x in turned.items()}

    def swap(x):
        return pltpu.roll(x, lanes // 2, 1)

    t1, c1, t2, c2 = {}, {}, {}, {}
    for i in range(ob):
        for k in range(ob):
            x1 = keep_ref[i, k]
            x2 = turned[i, k]
            denom = (e_ref[i] + e_ref[ob + k]) - vc_ref[...] - vall_ref[...]
            t1[i, k] = (x1 / denom).astype(BF)
            t2[i, k] = (x2 / denom).astype(BF)
            c1[i, k] = ((2.0 * x1 - x2) / denom).astype(BF)
            c2[i, k] = ((2.0 * x2 - x1) / denom).astype(BF)
    order = [(i, k) for i in range(ob) for k in range(ob)]
    amps = jnp.concatenate([t1[x] for x in order] + [t2[x] for x in order], axis=0)
    contra = jnp.concatenate([c1[x] for x in order] + [c2[x] for x in order], axis=0)
    vt = lax.dot_general(contra, amps, (((0,), (0,)), ((), ())), preferred_element_type=F32)
    split = vt.reshape(nvir // 16, 2, 8, nvir)
    h0 = split[:, 0].reshape(nvir // 2, nvir)
    h1 = split[:, 1].reshape(nvir // 2, nvir)
    low = lax.broadcasted_iota(jnp.int32, (nvir // 2, lanes), 1) < lanes // 2
    for j in range(nv // 2):
        x, y = h0[:, j * lanes : (j + 1) * lanes], h1[:, j * lanes : (j + 1) * lanes]
        o_ref[2 * j, : nvir // 2] = jnp.where(low, x, swap(y)).astype(o_ref.dtype)
        o_ref[2 * j + 1, : nvir // 2] = jnp.where(low, swap(x), y).astype(o_ref.dtype)

    def dot(x, y):
        rows = jnp.sum(x.astype(F32) * y.astype(F32), axis=0, keepdims=True)
        return sum(rows[:, j * lanes : (j + 1) * lanes] for j in range(nvir // lanes))

    occ = [-sum(dot(t1[i, k], c1[m, k]) for k in range(ob)) for i in range(ob) for m in range(ob)]
    occ += [-sum(dot(t2[i, k], c2[i, n]) for i in range(ob)) for k in range(ob) for n in range(ob)]
    occ = jnp.concatenate(occ, axis=0)
    high = occ.astype(BF)
    rest = (occ - high.astype(F32)).astype(BF)
    tail = jnp.concatenate([high, rest], axis=0).astype(o_ref.dtype)
    for v in range(nv):
        o_ref[v, nvir // 2 :] = tail


def density(energies, keep, turned, vc, vall):
    ranks, _, lanes = turned.shape
    nvir = vall.shape[1]
    return pl.pallas_call(
        density_kernel,
        out_shape=jax.ShapeDtypeStruct((ranks // 2, nvir // 2 + 16, lanes), BF),
        in_specs=[SMEM] + [VMEM] * 4,
        out_specs=VMEM,
        compiler_params=PARAMS,
    )(energies, keep, turned, vc, vall)


def lane_sum_kernel(at_ref, p_ref, o_ref):
    total = p_ref[0].astype(F32)
    for src in range(1, p_ref.shape[0]):
        total += p_ref[src].astype(F32)
    count = o_ref.shape[0]
    n = 8 * count
    occ = total[n : n + 8] + total[n + 8 : n + 16]
    other = pltpu.roll(occ, 4, 0)
    for o in range(count):
        o_ref[o, :8] = total[8 * o : 8 * o + 8]
        o_ref[o, 8:] = jnp.where(at_ref[0] == o, occ, jnp.where(at_ref[1] == o, other, 0.0))


def lane_sum(at, parts, count):
    return pl.pallas_call(
        lane_sum_kernel,
        out_shape=jax.ShapeDtypeStruct((count, 16, parts.shape[2]), F32),
        in_specs=[SMEM, VMEM],
        out_specs=VMEM,
        compiler_params=PARAMS,
    )(at, parts)


def last_sum_kernel(p_ref, occ_ref, vir_ref):
    total = p_ref[0]
    for src in range(1, p_ref.shape[0]):
        total += p_ref[src]
    turned = total[:8].T
    slab = turned.shape[0] // 2
    vir_ref[:, :8] = turned[:slab]
    vir_ref[:, 8:] = turned[slab:]
    occ = jnp.sum(total[8:], axis=1, keepdims=True)
    ob = occ_ref.shape[0]
    for i in range(ob):
        for m in range(ob):
            occ_ref[i : i + 1, m : m + 1] = occ[ob * i + m : ob * i + m + 1]


def last_sum(parts, ob, slab):
    return pl.pallas_call(
        last_sum_kernel,
        out_shape=[
            jax.ShapeDtypeStruct((ob, ob), F32),
            jax.ShapeDtypeStruct((slab, 16), F32),
        ],
        in_specs=[VMEM],
        out_specs=[VMEM, VMEM],
        compiler_params=PARAMS,
    )(parts)


def chip_groups(count, lanes):
    return [
        [(low + core) * lanes + v for v in range(lanes) for core in range(2)]
        for low in range(0, count, 2)
    ]


def by_chip(offset, count, branch, *operands):
    return lax.switch(offset, [functools.partial(branch, m) for m in range(count // 2)], *operands)


def per_device(three_index, occ_energy, vir_energy, partner):
    ob, slab, naux = three_index.shape
    nvir = vir_energy.shape[0]
    count, lanes = lax.axis_size("occ"), lax.axis_size("vir")
    p, v = lax.axis_index("occ"), lax.axis_index("vir")
    offset = jnp.bitwise_xor(p, partner[0])
    chip, core = p // 2, p % 2
    far, cross = offset // 2, offset % 2
    higher = chip > jnp.bitwise_xor(chip, far)
    stay_core = jnp.where(higher, 1 - cross, 0)
    stay = 2 * chip + stay_core
    come = jnp.bitwise_xor(stay, offset)
    half = slab // 2
    groups = chip_groups(count, lanes)

    def over_vir(x):
        return lax.all_to_all(x, "vir", 0, 0, tiled=True)

    def over_chips(x):
        return lax.all_to_all(x, BOTH, 0, 0, axis_index_groups=groups, tiled=True)

    def to_chip(m, x):
        return lax.ppermute(x, "occ", [(a, a ^ 2 * m) for a in range(count)]) if m else x

    def first_step(m, lead, rest):
        return to_chip(m, lead), over_vir(rest)

    def second_step(m, lead, last):
        return over_vir(lead), to_chip(m, last)

    at = jnp.stack([core, (core == stay_core).astype(jnp.int32)])
    other = lax.ppermute(cut(at, three_index, lanes), "occ", [(a, a ^ 1) for a in range(count)])
    lead, rest = pick(at, three_index, other)
    lead, mine = by_chip(far, count, first_step, lead, rest)
    come0, come1 = by_chip(far, count, second_step, lead, mine[:, 2])
    keep, turn = gather_sum(over_chips(product(mine, come0, come1, ob)))
    turned = over_chips(turn)
    energies = jnp.concatenate([
        lax.dynamic_slice_in_dim(occ_energy, stay * ob, ob),
        lax.dynamic_slice_in_dim(occ_energy, come * ob, ob),
    ])
    vc = lax.dynamic_slice_in_dim(vir_energy, v * slab + core * half, half)
    packed = density(energies, keep, turned, vc.reshape(half, 1), vir_energy.reshape(1, nvir))
    pieces = lane_sum(jnp.stack([stay, come]), over_vir(packed), count)
    return tuple(last_sum(lax.all_to_all(pieces, "occ", 0, 0, tiled=True), ob, slab))


def solution(mesh):
    in_specs = (P("occ", "vir", None), P(), P(), P("occ"))
    out_specs = (P("occ", None), P("vir", "occ"))
    return jax.shard_map(
        per_device, mesh=mesh, in_specs=in_specs, out_specs=out_specs, check_vma=False
    )
```

```python
import functools

import jax
import jax.numpy as jnp
from jax import lax
from jax.experimental import pallas as pl
from jax.experimental.pallas import tpu as pltpu
from jax.sharding import PartitionSpec as P

BF = jnp.bfloat16
F32 = jnp.float32
BOTH = ("occ", "vir")
SMEM = pl.BlockSpec(memory_space=pltpu.SMEM)
VMEM = pl.BlockSpec(memory_space=pltpu.VMEM)
ANY = pl.BlockSpec(memory_space=pl.ANY)
HBM = pl.BlockSpec(memory_space=pltpu.HBM)


def vmem(mib):
    return pltpu.CompilerParams(vmem_limit_bytes=mib * 1024 * 1024)


def cut_kernel(at_ref, x_ref, their0_ref, their1_ref, own_ref, sems):
    parts, _, q = own_ref.shape
    copies = []
    for w in range(parts):
        theirs = pl.multiple_of(((1 - at_ref[0]) * parts + w) * q, q)
        mine = pl.multiple_of((at_ref[0] * parts + w) * q, q)
        for n, (i, start, ref) in enumerate(
            [(0, theirs, their0_ref), (0, mine, own_ref), (1, theirs, their1_ref)]
        ):
            copies.append(
                pltpu.make_async_copy(x_ref.at[i, :, pl.ds(start, q)], ref.at[w], sems.at[w, n])
            )
    for c in copies:
        c.start()
    for c in copies:
        c.wait()


def cut(at, x, parts):
    _, slab, naux = x.shape
    q = naux // (2 * parts)
    return pl.pallas_call(
        cut_kernel,
        out_shape=[jax.ShapeDtypeStruct((parts, slab, q), x.dtype)] * 3,
        in_specs=[SMEM, HBM],
        out_specs=[VMEM] * 3,
        scratch_shapes=[pltpu.SemaphoreType.DMA((parts, 3))],
        compiler_params=vmem(8),
    )(at, x)


def pick_kernel(at_ref, x_ref, other0_ref, other1_ref, o_ref, sems):
    parts, _, _, q = o_ref.shape

    def fill(stays):
        copies = []
        for w in range(parts):
            start = pl.multiple_of((at_ref[0] * parts + w) * q, q)
            own = [x_ref.at[n, :, pl.ds(start, q)] for n in range(2)]
            other = [other0_ref.at[w], other1_ref.at[w]]
            stay, leave = (own, other) if stays else (other, own)
            for n, src in enumerate([stay[0], stay[1], leave[1]]):
                copies.append(pltpu.make_async_copy(src, o_ref.at[w, n], sems.at[w, n]))
        for c in copies:
            c.start()
        for c in copies:
            c.wait()

    pl.when(at_ref[1] != 0)(lambda: fill(True))
    pl.when(at_ref[1] == 0)(lambda: fill(False))


def pick(at, x, other0, other1):
    parts, slab, q = other0.shape
    return pl.pallas_call(
        pick_kernel,
        out_shape=jax.ShapeDtypeStruct((parts, 3, slab, q), x.dtype),
        in_specs=[SMEM, HBM, ANY, ANY],
        out_specs=VMEM,
        scratch_shapes=[pltpu.SemaphoreType.DMA((parts, 3))],
        compiler_params=vmem(8),
    )(at, x, other0, other1)


def product_kernel(at_ref, mine_ref, come0_ref, come1_ref, own_ref, other_ref):
    nv, ob, slab, q = mine_ref.shape
    n = nv * slab
    half = own_ref.shape[2]
    first = at_ref[0] == 0
    for k, come_ref in enumerate((come0_ref, come1_ref)):
        cols = come_ref[...].reshape(n, q)
        for i in range(ob):
            rows = mine_ref[:, i].reshape(n, q)
            out = lax.dot_general(rows, cols, (((1,), (1,)), ((), ())), preferred_element_type=F32)
            out = out.reshape(nv, 2, half, n)
            own_ref[:, i, :, k * n : (k + 1) * n] = jnp.where(first, out[:, 0], out[:, 1])
            other_ref[:, i, :, k * n : (k + 1) * n] = jnp.where(first, out[:, 1], out[:, 0]).astype(BF)


def product(at, mine, come0, come1, ob):
    nv, slab, q = come0.shape
    shape = (nv, ob, slab // 2, ob * nv * slab)
    come = pl.BlockSpec((nv, slab, q), lambda r: (0, 0, 0))
    whole = pl.BlockSpec(shape, lambda r: (0, 0, 0, 0))
    return pl.pallas_call(
        product_kernel,
        grid=(1,),
        out_shape=[jax.ShapeDtypeStruct(shape, F32), jax.ShapeDtypeStruct(shape, BF)],
        in_specs=[SMEM, pl.BlockSpec((nv, ob, slab, q), lambda r: (0, 0, 0, 0)), come, come],
        out_specs=[whole, whole],
        compiler_params=vmem(24),
    )(at, mine, come0, come1)


def core_sum_kernel(own_ref, other_ref, o_ref):
    o_ref[...] = (own_ref[...] + other_ref[...].astype(F32)).astype(BF)


def core_sum(own, other):
    nv, ob, half, cols = own.shape
    spec = pl.BlockSpec((2, ob, half, cols), lambda r: (r, 0, 0, 0))
    return pl.pallas_call(
        core_sum_kernel,
        grid=(nv // 2,),
        out_shape=jax.ShapeDtypeStruct(own.shape, BF),
        in_specs=[spec, spec],
        out_specs=spec,
        compiler_params=vmem(8),
    )(own, other)


def gather_sum_kernel(p0_ref, p1_ref, keep_ref, turn_ref):
    rows = []
    for k, ref in enumerate((p0_ref, p1_ref)):
        total = ref[0].astype(F32)
        for src in range(1, ref.shape[0]):
            total += ref[src].astype(F32)
        keep_ref[:, k] = total
        rows.append(total.reshape(-1, total.shape[2]))
    turned = jnp.concatenate(rows, axis=0).T
    turn_ref[...] = turned.reshape(turn_ref.shape).astype(BF)


def gather_sum(parts):
    ranks, ob, half, cols = parts.shape
    nvir, lanes = cols // ob, 2 * ob * half
    steps = nvir // lanes
    return pl.pallas_call(
        gather_sum_kernel,
        grid=(steps,),
        out_shape=[
            jax.ShapeDtypeStruct((ob, ob, half, nvir), F32),
            jax.ShapeDtypeStruct((nvir // half, half, lanes), BF),
        ],
        in_specs=[
            pl.BlockSpec((ranks, ob, half, lanes), lambda j: (0, 0, 0, j)),
            pl.BlockSpec((ranks, ob, half, lanes), lambda j: (0, 0, 0, j + steps)),
        ],
        out_specs=[
            pl.BlockSpec((ob, ob, half, lanes), lambda j: (0, 0, 0, j)),
            pl.BlockSpec((lanes // half, half, lanes), lambda j: (j, 0, 0)),
        ],
        compiler_params=vmem(8),
    )(parts, parts)


def density_kernel(e_ref, keep_ref, turn_ref, vc_ref, vall_ref, o_ref):
    ob, _, half, nvir = keep_ref.shape
    ranks, _, lanes = turn_ref.shape
    nv = ranks // 2
    spots = lanes // half
    spot = lax.broadcasted_iota(jnp.int32, (half, lanes), 1) // half
    turned = {}
    for g in range(ranks // spots):
        moved = []
        for j in range(spots):
            x = turn_ref[g * spots + j].astype(F32)
            moved.append([x] + [pltpu.roll(x, n * half, 1) for n in range(1, spots)])
        for ki in range(spots):
            whole = moved[0][(-ki) % spots]
            for j in range(1, spots):
                whole = jnp.where(spot == j, moved[j][(j - ki) % spots], whole)
            turned.setdefault((ki % ob, ki // ob), []).append(whole)
    turned = {ik: jnp.concatenate(x, axis=1) for ik, x in turned.items()}

    def swap(x):
        return pltpu.roll(x, lanes // 2, 1)

    t1, c1, t2, c2 = {}, {}, {}, {}
    for i in range(ob):
        for k in range(ob):
            x1 = keep_ref[i, k]
            x2 = turned[i, k]
            denom = (e_ref[i] + e_ref[ob + k]) - vc_ref[...] - vall_ref[...]
            t1[i, k] = (x1 / denom).astype(BF)
            t2[i, k] = (x2 / denom).astype(BF)
            c1[i, k] = ((2.0 * x1 - x2) / denom).astype(BF)
            c2[i, k] = ((2.0 * x2 - x1) / denom).astype(BF)
    order = [(i, k) for i in range(ob) for k in range(ob)]
    amps = jnp.concatenate([t1[x] for x in order] + [t2[x] for x in order], axis=0)
    contra = jnp.concatenate([c1[x] for x in order] + [c2[x] for x in order], axis=0)
    vt = lax.dot_general(contra, amps, (((0,), (0,)), ((), ())), preferred_element_type=F32)
    split = vt.reshape(nvir // 16, 2, 8, nvir)
    h0 = split[:, 0].reshape(nvir // 2, nvir)
    h1 = split[:, 1].reshape(nvir // 2, nvir)
    low = lax.broadcasted_iota(jnp.int32, (nvir // 2, lanes), 1) < lanes // 2
    for j in range(nv // 2):
        x, y = h0[:, j * lanes : (j + 1) * lanes], h1[:, j * lanes : (j + 1) * lanes]
        o_ref[2 * j, : nvir // 2] = jnp.where(low, x, swap(y)).astype(o_ref.dtype)
        o_ref[2 * j + 1, : nvir // 2] = jnp.where(low, swap(x), y).astype(o_ref.dtype)

    def dot(x, y):
        rows = jnp.sum(x.astype(F32) * y.astype(F32), axis=0, keepdims=True)
        return sum(rows[:, j * lanes : (j + 1) * lanes] for j in range(nvir // lanes))

    occ = [-sum(dot(t1[i, k], c1[m, k]) for k in range(ob)) for i in range(ob) for m in range(ob)]
    occ += [-sum(dot(t2[i, k], c2[i, n]) for i in range(ob)) for k in range(ob) for n in range(ob)]
    occ = jnp.concatenate(occ, axis=0)
    high = occ.astype(BF)
    rest = (occ - high.astype(F32)).astype(BF)
    tail = jnp.concatenate([high, rest], axis=0).astype(o_ref.dtype)
    for v in range(nv):
        o_ref[v, nvir // 2 :] = tail


def density(energies, keep, turned, vc, vall):
    ranks, _, lanes = turned.shape
    nvir = vall.shape[1]
    return pl.pallas_call(
        density_kernel,
        out_shape=jax.ShapeDtypeStruct((ranks // 2, nvir // 2 + 16, lanes), BF),
        in_specs=[SMEM] + [VMEM] * 4,
        out_specs=VMEM,
        compiler_params=vmem(16),
    )(energies, keep, turned, vc, vall)


def lane_sum_kernel(at_ref, p_ref, o_ref):
    total = p_ref[0].astype(F32)
    for src in range(1, p_ref.shape[0]):
        total += p_ref[src].astype(F32)
    count = o_ref.shape[0]
    n = 8 * count
    occ = total[n : n + 8] + total[n + 8 : n + 16]
    other = pltpu.roll(occ, 4, 0)
    for o in range(count):
        o_ref[o, :8] = total[8 * o : 8 * o + 8]
        o_ref[o, 8:] = jnp.where(at_ref[0] == o, occ, jnp.where(at_ref[1] == o, other, 0.0))


def lane_sum(at, parts, count):
    return pl.pallas_call(
        lane_sum_kernel,
        out_shape=jax.ShapeDtypeStruct((count, 16, parts.shape[2]), F32),
        in_specs=[SMEM, VMEM],
        out_specs=VMEM,
        compiler_params=vmem(8),
    )(at, parts)


def last_sum_kernel(p_ref, occ_ref, vir_ref):
    total = p_ref[0]
    for src in range(1, p_ref.shape[0]):
        total += p_ref[src]
    slab = vir_ref.shape[1]
    vir_ref[:8] = total[:8, :slab]
    vir_ref[8:] = total[:8, slab:]
    occ = jnp.sum(total[8:], axis=1, keepdims=True)
    ob = occ_ref.shape[0]
    for i in range(ob):
        for m in range(ob):
            occ_ref[i : i + 1, m : m + 1] = occ[ob * i + m : ob * i + m + 1]


def last_sum(parts, ob, slab):
    return pl.pallas_call(
        last_sum_kernel,
        out_shape=[
            jax.ShapeDtypeStruct((ob, ob), F32),
            jax.ShapeDtypeStruct((16, slab), F32),
        ],
        in_specs=[VMEM],
        out_specs=[VMEM, VMEM],
        compiler_params=vmem(4),
    )(parts)


def chip_groups(count, lanes):
    return [
        [(low + core) * lanes + v for v in range(lanes) for core in range(2)]
        for low in range(0, count, 2)
    ]


def by_chip(offset, count, branch, *operands):
    return lax.switch(offset, [functools.partial(branch, m) for m in range(count // 2)], *operands)


def per_device(three_index, occ_energy, vir_energy, partner):
    ob, slab, naux = three_index.shape
    nvir = vir_energy.shape[0]
    count, lanes = lax.axis_size("occ"), lax.axis_size("vir")
    p, v = lax.axis_index("occ"), lax.axis_index("vir")
    offset = jnp.bitwise_xor(p, partner[0])
    chip, core = p // 2, p % 2
    far, cross = offset // 2, offset % 2
    higher = chip > jnp.bitwise_xor(chip, far)
    stay_core = jnp.where(higher, 1 - cross, 0)
    stay = 2 * chip + stay_core
    come = jnp.bitwise_xor(stay, offset)
    half = slab // 2
    groups = chip_groups(count, lanes)

    def over_vir(x):
        return lax.all_to_all(x, "vir", 0, 0, tiled=True)

    def over_chips(x):
        return lax.all_to_all(x, BOTH, 0, 0, axis_index_groups=groups, tiled=True)

    def to_chip(m, x):
        return lax.ppermute(x, "occ", [(a, a ^ 2 * m) for a in range(count)]) if m else x

    def to_sibling(x):
        return lax.ppermute(x, "occ", [(a, a ^ 1) for a in range(count)])

    def exchange(m, at, x, other0, other1, lead):
        def spread(*operands):
            return over_vir(pick(*operands))

        def never(at, x, other0, other1):
            return jnp.zeros((lanes, 3) + other0.shape[1:], x.dtype)

        lead = to_chip(m, lead)
        mine = lax.cond(partner[0] >= 0, spread, never, at, x, other0, other1)
        last = to_chip(m, mine[:, 2])
        lead, mine = lax.optimization_barrier((lead, mine))
        return mine, over_vir(lead), last

    at = jnp.stack([core, (core == stay_core).astype(jnp.int32)])
    their0, their1, lead = cut(at, three_index, lanes)
    other0, other1 = to_sibling(their0), to_sibling(their1)
    lead = jnp.where(core == stay_core, other0, lead)
    mine, come0, come1 = by_chip(far, count, exchange, at, three_index, other0, other1, lead)
    own, others = product(at, mine, come0, come1, ob)
    keep, turn = gather_sum(over_vir(core_sum(own, to_sibling(others))))
    turned = over_chips(turn)
    energies = jnp.concatenate([
        lax.dynamic_slice_in_dim(occ_energy, stay * ob, ob),
        lax.dynamic_slice_in_dim(occ_energy, come * ob, ob),
    ])
    vc = lax.dynamic_slice_in_dim(vir_energy, v * slab + core * half, half)
    packed = density(energies, keep, turned, vc.reshape(half, 1), vir_energy.reshape(1, nvir))
    pieces = lane_sum(jnp.stack([stay, come]), over_vir(packed), count)
    occ_density, vir_turned = last_sum(lax.all_to_all(pieces, "occ", 0, 0, tiled=True), ob, slab)
    return occ_density, vir_turned.T


def solution(mesh):
    in_specs = (P("occ", "vir", None), P(), P(), P("occ"))
    out_specs = (P("occ", None), P("vir", "occ"))
    return jax.shard_map(
        per_device, mesh=mesh, in_specs=in_specs, out_specs=out_specs, check_vma=False
    )
```

```python
import functools

import jax
import jax.numpy as jnp
from jax import lax
from jax.experimental import pallas as pl
from jax.experimental.pallas import tpu as pltpu
from jax.sharding import PartitionSpec as P

BF = jnp.bfloat16
F32 = jnp.float32
BOTH = ("occ", "vir")
SMEM = pl.BlockSpec(memory_space=pltpu.SMEM)
VMEM = pl.BlockSpec(memory_space=pltpu.VMEM)
ANY = pl.BlockSpec(memory_space=pl.ANY)
HBM = pl.BlockSpec(memory_space=pltpu.HBM)


def vmem(mib):
    return pltpu.CompilerParams(vmem_limit_bytes=mib * 1024 * 1024)


def copy_all(parts, copies_of, sems):
    def each(w, begin):
        for n, (src, dst) in enumerate(copies_of(w)):
            copy = pltpu.make_async_copy(src, dst, sems.at[w, n])
            copy.start() if begin else copy.wait()

    lax.fori_loop(0, parts, lambda w, _: each(w, True), None)
    lax.fori_loop(0, parts, lambda w, _: each(w, False), None)


def cut_kernel(at_ref, x_ref, their0_ref, their1_ref, own_ref, sems):
    parts, lead, q = own_ref.shape
    slab = x_ref.shape[1]
    more = lead - slab

    def copies_of(w):
        theirs = pl.ds(pl.multiple_of(((1 - at_ref[0]) * parts + w) * q, q), q)
        mine = pl.ds(pl.multiple_of((at_ref[0] * parts + w) * q, q), q)
        copies = [
            (x_ref.at[0, :, theirs], their0_ref.at[w, :slab]),
            (x_ref.at[1, more:, theirs], their1_ref.at[w]),
            (x_ref.at[0, :, mine], own_ref.at[w, :slab]),
        ]
        if more:
            copies += [
                (x_ref.at[1, :more, theirs], their0_ref.at[w, slab:]),
                (x_ref.at[1, :more, mine], own_ref.at[w, slab:]),
            ]
        return copies

    copy_all(parts, copies_of, sems)


def cut(at, x, parts, lead):
    ob, slab, naux = x.shape
    q = naux // (2 * parts)
    return pl.pallas_call(
        cut_kernel,
        out_shape=[
            jax.ShapeDtypeStruct((parts, rows, q), x.dtype)
            for rows in (lead, ob * slab - lead, lead)
        ],
        in_specs=[SMEM, HBM],
        out_specs=[VMEM] * 3,
        scratch_shapes=[pltpu.SemaphoreType.DMA((parts, 5))],
        compiler_params=vmem(8),
    )(at, x)


def pick_kernel(at_ref, x_ref, other0_ref, other1_ref, o_ref, sems):
    parts, rows, q = o_ref.shape
    lead, last = other0_ref.shape[1], other1_ref.shape[1]
    slab = x_ref.shape[1]
    more = lead - slab

    def fill(stays):
        def copies_of(w):
            mine = pl.ds(pl.multiple_of((at_ref[0] * parts + w) * q, q), q)
            if stays:
                return [
                    (x_ref.at[0, :, mine], o_ref.at[w, :slab]),
                    (x_ref.at[1, :, mine], o_ref.at[w, slab : 2 * slab]),
                    (other1_ref.at[w], o_ref.at[w, 2 * slab :]),
                ]
            return [
                (other0_ref.at[w], o_ref.at[w, :lead]),
                (other1_ref.at[w], o_ref.at[w, lead : lead + last]),
                (x_ref.at[1, more:, mine], o_ref.at[w, 2 * slab :]),
            ]

        copy_all(parts, copies_of, sems)

    pl.when(at_ref[1] != 0)(lambda: fill(True))
    pl.when(at_ref[1] == 0)(lambda: fill(False))


def pick(at, x, other0, other1):
    parts, lead, q = other0.shape
    last = other1.shape[1]
    return pl.pallas_call(
        pick_kernel,
        out_shape=jax.ShapeDtypeStruct((parts, lead + 2 * last, q), x.dtype),
        in_specs=[SMEM, HBM, ANY, ANY],
        out_specs=VMEM,
        scratch_shapes=[pltpu.SemaphoreType.DMA((parts, 3))],
        compiler_params=vmem(8),
    )(at, x, other0, other1)


def product_kernel(at_ref, mine_ref, come0_ref, come1_ref, own_ref, other_ref):
    nv, lead, q = come0_ref.shape
    _, ob, half, _ = own_ref.shape
    slab = 2 * half
    n = nv * slab
    first = at_ref[0] == 0
    blocks = [come0_ref[:, :slab], come1_ref[...]]
    if lead > slab:
        blocks[1] = jnp.concatenate([come0_ref[:, slab:], blocks[1]], axis=1)
    for k, block in enumerate(blocks):
        cols = block.reshape(n, q)
        for i in range(ob):
            rows = mine_ref[:, i * slab : (i + 1) * slab].reshape(n, q)
            out = lax.dot_general(rows, cols, (((1,), (1,)), ((), ())), preferred_element_type=F32)
            out = out.reshape(nv, 2, half, n)
            own_ref[:, i, :, k * n : (k + 1) * n] = jnp.where(first, out[:, 0], out[:, 1])
            other_ref[:, i, :, k * n : (k + 1) * n] = jnp.where(first, out[:, 1], out[:, 0]).astype(BF)


def product(at, mine, come0, come1, ob, slab):
    nv = mine.shape[0]
    shape = (nv, ob, slab // 2, ob * nv * slab)
    return pl.pallas_call(
        product_kernel,
        out_shape=[jax.ShapeDtypeStruct(shape, F32), jax.ShapeDtypeStruct(shape, BF)],
        in_specs=[SMEM, VMEM, VMEM, VMEM],
        out_specs=[VMEM, VMEM],
        compiler_params=vmem(24),
    )(at, mine, come0, come1)


def core_sum_kernel(own_ref, other_ref, o_ref):
    o_ref[...] = (own_ref[...] + other_ref[...].astype(F32)).astype(BF)


def core_sum(own, other):
    nv, ob, half, cols = own.shape
    spec = pl.BlockSpec((2, ob, half, cols), lambda r: (r, 0, 0, 0))
    return pl.pallas_call(
        core_sum_kernel,
        grid=(nv // 2,),
        out_shape=jax.ShapeDtypeStruct(own.shape, BF),
        in_specs=[spec, spec],
        out_specs=spec,
        compiler_params=vmem(8),
    )(own, other)


def gather_sum_kernel(p0_ref, p1_ref, keep_ref, turn_ref):
    rows = []
    for k, ref in enumerate((p0_ref, p1_ref)):
        total = ref[0].astype(F32)
        for src in range(1, ref.shape[0]):
            total += ref[src].astype(F32)
        keep_ref[:, k] = total
        rows.append(total.reshape(-1, total.shape[2]))
    turned = jnp.concatenate(rows, axis=0).T
    turn_ref[...] = turned.reshape(turn_ref.shape).astype(BF)


def gather_sum(parts):
    ranks, ob, half, cols = parts.shape
    nvir, lanes = cols // ob, 2 * ob * half
    steps = nvir // lanes
    return pl.pallas_call(
        gather_sum_kernel,
        grid=(steps,),
        out_shape=[
            jax.ShapeDtypeStruct((ob, ob, half, nvir), F32),
            jax.ShapeDtypeStruct((nvir // half, half, lanes), BF),
        ],
        in_specs=[
            pl.BlockSpec((ranks, ob, half, lanes), lambda j: (0, 0, 0, j)),
            pl.BlockSpec((ranks, ob, half, lanes), lambda j: (0, 0, 0, j + steps)),
        ],
        out_specs=[
            pl.BlockSpec((ob, ob, half, lanes), lambda j: (0, 0, 0, j)),
            pl.BlockSpec((lanes // half, half, lanes), lambda j: (j, 0, 0)),
        ],
        compiler_params=vmem(8),
    )(parts, parts)


def density_kernel(e_ref, keep_ref, turn_ref, vc_ref, vall_ref, o_ref):
    ob, _, half, nvir = keep_ref.shape
    ranks, _, lanes = turn_ref.shape
    nv = ranks // 2
    spots = lanes // half
    spot = lax.broadcasted_iota(jnp.int32, (half, lanes), 1) // half
    turned = {}
    for g in range(ranks // spots):
        moved = []
        for j in range(spots):
            x = turn_ref[g * spots + j].astype(F32)
            moved.append([x] + [pltpu.roll(x, n * half, 1) for n in range(1, spots)])
        for ki in range(spots):
            whole = moved[0][(-ki) % spots]
            for j in range(1, spots):
                whole = jnp.where(spot == j, moved[j][(j - ki) % spots], whole)
            turned.setdefault((ki % ob, ki // ob), []).append(whole)
    turned = {ik: jnp.concatenate(x, axis=1) for ik, x in turned.items()}

    def swap(x):
        return pltpu.roll(x, lanes // 2, 1)

    t1, c1, t2, c2 = {}, {}, {}, {}
    for i in range(ob):
        for k in range(ob):
            x1 = keep_ref[i, k]
            x2 = turned[i, k]
            denom = (e_ref[i] + e_ref[ob + k]) - vc_ref[...] - vall_ref[...]
            t1[i, k] = (x1 / denom).astype(BF)
            t2[i, k] = (x2 / denom).astype(BF)
            c1[i, k] = ((2.0 * x1 - x2) / denom).astype(BF)
            c2[i, k] = ((2.0 * x2 - x1) / denom).astype(BF)
    order = [(i, k) for i in range(ob) for k in range(ob)]
    amps = jnp.concatenate([t1[x] for x in order] + [t2[x] for x in order], axis=0)
    contra = jnp.concatenate([c1[x] for x in order] + [c2[x] for x in order], axis=0)
    vt = lax.dot_general(contra, amps, (((0,), (0,)), ((), ())), preferred_element_type=F32)
    split = vt.reshape(nvir // 16, 2, 8, nvir)
    h0 = split[:, 0].reshape(nvir // 2, nvir)
    h1 = split[:, 1].reshape(nvir // 2, nvir)
    low = lax.broadcasted_iota(jnp.int32, (nvir // 2, lanes), 1) < lanes // 2
    for j in range(nv // 2):
        x, y = h0[:, j * lanes : (j + 1) * lanes], h1[:, j * lanes : (j + 1) * lanes]
        o_ref[2 * j, : nvir // 2] = jnp.where(low, x, swap(y)).astype(o_ref.dtype)
        o_ref[2 * j + 1, : nvir // 2] = jnp.where(low, swap(x), y).astype(o_ref.dtype)

    def dot(x, y):
        rows = jnp.sum(x.astype(F32) * y.astype(F32), axis=0, keepdims=True)
        return sum(rows[:, j * lanes : (j + 1) * lanes] for j in range(nvir // lanes))

    occ = [-sum(dot(t1[i, k], c1[m, k]) for k in range(ob)) for i in range(ob) for m in range(ob)]
    occ += [-sum(dot(t2[i, k], c2[i, n]) for i in range(ob)) for k in range(ob) for n in range(ob)]
    occ = jnp.concatenate(occ, axis=0)
    high = occ.astype(BF)
    rest = (occ - high.astype(F32)).astype(BF)
    tail = jnp.concatenate([high, rest], axis=0).astype(o_ref.dtype)
    for v in range(nv):
        o_ref[v, nvir // 2 :] = tail


def density(energies, keep, turned, vc, vall):
    ranks, _, lanes = turned.shape
    nvir = vall.shape[1]
    return pl.pallas_call(
        density_kernel,
        out_shape=jax.ShapeDtypeStruct((ranks // 2, nvir // 2 + 16, lanes), BF),
        in_specs=[SMEM] + [VMEM] * 4,
        out_specs=VMEM,
        compiler_params=vmem(16),
    )(energies, keep, turned, vc, vall)


def lane_sum_kernel(at_ref, p_ref, o_ref):
    total = p_ref[0].astype(F32)
    for src in range(1, p_ref.shape[0]):
        total += p_ref[src].astype(F32)
    count = o_ref.shape[0]
    n = 8 * count
    occ = total[n : n + 8] + total[n + 8 : n + 16]
    other = pltpu.roll(occ, 4, 0)
    for o in range(count):
        o_ref[o, :8] = total[8 * o : 8 * o + 8]
        o_ref[o, 8:] = jnp.where(at_ref[0] == o, occ, jnp.where(at_ref[1] == o, other, 0.0))


def lane_sum(at, parts, count):
    return pl.pallas_call(
        lane_sum_kernel,
        out_shape=jax.ShapeDtypeStruct((count, 16, parts.shape[2]), F32),
        in_specs=[SMEM, VMEM],
        out_specs=VMEM,
        compiler_params=vmem(8),
    )(at, parts)


def last_sum_kernel(p_ref, occ_ref, vir_ref):
    total = p_ref[0]
    for src in range(1, p_ref.shape[0]):
        total += p_ref[src]
    slab = vir_ref.shape[1]
    vir_ref[:8] = total[:8, :slab]
    vir_ref[8:] = total[:8, slab:]
    occ = jnp.sum(total[8:], axis=1, keepdims=True)
    ob = occ_ref.shape[0]
    for i in range(ob):
        for m in range(ob):
            occ_ref[i : i + 1, m : m + 1] = occ[ob * i + m : ob * i + m + 1]


def last_sum(parts, ob, slab):
    return pl.pallas_call(
        last_sum_kernel,
        out_shape=[
            jax.ShapeDtypeStruct((ob, ob), F32),
            jax.ShapeDtypeStruct((16, slab), F32),
        ],
        in_specs=[VMEM],
        out_specs=[VMEM, VMEM],
        compiler_params=vmem(4),
    )(parts)


def chip_groups(count, lanes):
    return [
        [(low + core) * lanes + v for v in range(lanes) for core in range(2)]
        for low in range(0, count, 2)
    ]


def by_chip(offset, count, branch, *operands):
    return lax.switch(offset, [functools.partial(branch, m) for m in range(count // 2)], *operands)


def per_device(three_index, occ_energy, vir_energy, partner):
    ob, slab, naux = three_index.shape
    nvir = vir_energy.shape[0]
    count, lanes = lax.axis_size("occ"), lax.axis_size("vir")
    p, v = lax.axis_index("occ"), lax.axis_index("vir")
    offset = jnp.bitwise_xor(p, partner[0])
    chip, core = p // 2, p % 2
    far, cross = offset // 2, offset % 2
    higher = chip > jnp.bitwise_xor(chip, far)
    stay_core = jnp.where(higher, 1 - cross, 0)
    stay = 2 * chip + stay_core
    come = jnp.bitwise_xor(stay, offset)
    half = slab // 2
    groups = chip_groups(count, lanes)

    def over_vir(x):
        return lax.all_to_all(x, "vir", 0, 0, tiled=True)

    def over_chips(x):
        return lax.all_to_all(x, BOTH, 0, 0, axis_index_groups=groups, tiled=True)

    def to_chip(m, x, turn=0):
        route = [
            (a * lanes + w, (a ^ 2 * m) * lanes + (w ^ turn)) for a in range(count) for w in range(lanes)
        ]
        return lax.ppermute(x, BOTH, route) if m else x

    def to_sibling(x):
        return lax.ppermute(x, "occ", [(a, a ^ 1) for a in range(count)])

    row = lanes // 2
    upper = v // row

    def by_half(m):
        return m // (count // 4) == 1 and m % (count // 4) < 2

    def lead_on(m, x):
        if not by_half(m):
            return (to_chip(m, x),)
        stay = lax.dynamic_slice_in_dim(x, upper * row, row)
        turn = lax.dynamic_slice_in_dim(x, (1 - upper) * row, row)
        return to_chip(m, stay), to_chip(m, turn, row)

    def lead_over(m, straight, *turned):
        if not turned:
            return over_vir(straight)
        (turned,) = turned
        flip = upper == 1
        both = jnp.stack(
            [jnp.where(flip, turned, straight), jnp.where(flip, straight, turned)], axis=1
        )
        halves = [list(range(row)), list(range(row, lanes))]
        both = lax.all_to_all(both, "vir", 0, 0, axis_index_groups=halves, tiled=True)
        return jnp.swapaxes(both, 0, 1).reshape((lanes,) + both.shape[2:])

    def exchange(m, at, x, other0, other1, lead):
        def step(run, *operands):
            like = jax.eval_shape(run, *operands)
            never = lambda *_: jax.tree.map(lambda y: jnp.zeros(y.shape, y.dtype), like)
            return lax.cond(partner[0] >= 0, run, never, *operands)

        def spread(*operands):
            mine = over_vir(pick(*operands))
            return mine, mine[:, ob * slab :]

        lead = lead_on(m, lead)
        mine, last = step(spread, at, x, other0, other1)
        if by_half(m):
            lead, last = lax.optimization_barrier((lead, last))
        last = to_chip(m, last)
        lead, mine = lax.optimization_barrier((lead, mine))
        return mine, step(functools.partial(lead_over, m), *lead), last

    lead_rows = slab + slab // 4
    last_rows = ob * slab - lead_rows
    at = jnp.stack([core, (core == stay_core).astype(jnp.int32)])
    their0, their1, lead = cut(at, three_index, lanes, lead_rows)
    other0, other1 = to_sibling(their0), to_sibling(their1)
    lead = jnp.where(core == stay_core, other0, lead)
    mine, come0, come1 = by_chip(far, count, exchange, at, three_index, other0, other1, lead)
    own, others = product(at, mine, come0, come1, ob, slab)
    keep, turn = gather_sum(over_vir(core_sum(own, to_sibling(others))))
    turned = over_chips(turn)
    energies = jnp.concatenate([
        lax.dynamic_slice_in_dim(occ_energy, stay * ob, ob),
        lax.dynamic_slice_in_dim(occ_energy, come * ob, ob),
    ])
    vc = lax.dynamic_slice_in_dim(vir_energy, v * slab + core * half, half)
    packed = density(energies, keep, turned, vc.reshape(half, 1), vir_energy.reshape(1, nvir))
    pieces = lane_sum(jnp.stack([stay, come]), over_vir(packed), count)
    occ_density, vir_turned = last_sum(lax.all_to_all(pieces, "occ", 0, 0, tiled=True), ob, slab)
    return occ_density, vir_turned.T


def solution(mesh):
    in_specs = (P("occ", "vir", None), P(), P(), P("occ"))
    out_specs = (P("occ", None), P("vir", "occ"))
    return jax.shard_map(
        per_device, mesh=mesh, in_specs=in_specs, out_specs=out_specs, check_vma=False
    )
```

```python
import functools

import jax
import jax.numpy as jnp
from jax import lax
from jax.experimental import pallas as pl
from jax.experimental.pallas import tpu as pltpu
from jax.sharding import PartitionSpec as P

BF = jnp.bfloat16
F32 = jnp.float32
BOTH = ("occ", "vir")
SMEM = pl.BlockSpec(memory_space=pltpu.SMEM)
VMEM = pl.BlockSpec(memory_space=pltpu.VMEM)
ANY = pl.BlockSpec(memory_space=pl.ANY)
HBM = pl.BlockSpec(memory_space=pltpu.HBM)


def vmem(mib):
    return pltpu.CompilerParams(vmem_limit_bytes=mib * 1024 * 1024)


def copy_all(parts, copies_of, sems):
    def each(w, begin):
        for n, (src, dst) in enumerate(copies_of(w)):
            copy = pltpu.make_async_copy(src, dst, sems.at[w, n])
            copy.start() if begin else copy.wait()

    lax.fori_loop(0, parts, lambda w, _: each(w, True), None)
    lax.fori_loop(0, parts, lambda w, _: each(w, False), None)


def cut_kernel(at_ref, x_ref, their0_ref, their1_ref, own_ref, sems):
    parts, lead, q = own_ref.shape
    slab = x_ref.shape[1]
    more = lead - slab

    def copies_of(w):
        theirs = pl.ds(pl.multiple_of(((1 - at_ref[0]) * parts + w) * q, q), q)
        mine = pl.ds(pl.multiple_of((at_ref[0] * parts + w) * q, q), q)
        copies = [
            (x_ref.at[0, :, theirs], their0_ref.at[w, :slab]),
            (x_ref.at[1, more:, theirs], their1_ref.at[w]),
            (x_ref.at[0, :, mine], own_ref.at[w, :slab]),
        ]
        if more:
            copies += [
                (x_ref.at[1, :more, theirs], their0_ref.at[w, slab:]),
                (x_ref.at[1, :more, mine], own_ref.at[w, slab:]),
            ]
        return copies

    copy_all(parts, copies_of, sems)


def cut(at, x, parts, lead):
    ob, slab, naux = x.shape
    q = naux // (2 * parts)
    return pl.pallas_call(
        cut_kernel,
        out_shape=[
            jax.ShapeDtypeStruct((parts, rows, q), x.dtype)
            for rows in (lead, ob * slab - lead, lead)
        ],
        in_specs=[SMEM, HBM],
        out_specs=[VMEM] * 3,
        scratch_shapes=[pltpu.SemaphoreType.DMA((parts, 5))],
        compiler_params=vmem(8),
    )(at, x)


def pick_kernel(at_ref, x_ref, other0_ref, other1_ref, o_ref, sems):
    parts, rows, q = o_ref.shape
    lead, last = other0_ref.shape[1], other1_ref.shape[1]
    slab = x_ref.shape[1]
    more = lead - slab

    def fill(stays):
        def copies_of(w):
            mine = pl.ds(pl.multiple_of((at_ref[0] * parts + w) * q, q), q)
            if stays:
                return [
                    (x_ref.at[0, :, mine], o_ref.at[w, :slab]),
                    (x_ref.at[1, :, mine], o_ref.at[w, slab : 2 * slab]),
                    (other1_ref.at[w], o_ref.at[w, 2 * slab :]),
                ]
            return [
                (other0_ref.at[w], o_ref.at[w, :lead]),
                (other1_ref.at[w], o_ref.at[w, lead : lead + last]),
                (x_ref.at[1, more:, mine], o_ref.at[w, 2 * slab :]),
            ]

        copy_all(parts, copies_of, sems)

    pl.when(at_ref[1] != 0)(lambda: fill(True))
    pl.when(at_ref[1] == 0)(lambda: fill(False))


def pick(at, x, other0, other1):
    parts, lead, q = other0.shape
    last = other1.shape[1]
    return pl.pallas_call(
        pick_kernel,
        out_shape=jax.ShapeDtypeStruct((parts, lead + 2 * last, q), x.dtype),
        in_specs=[SMEM, HBM, ANY, ANY],
        out_specs=VMEM,
        scratch_shapes=[pltpu.SemaphoreType.DMA((parts, 3))],
        compiler_params=vmem(8),
    )(at, x, other0, other1)


def product_kernel(at_ref, mine_ref, come0_ref, come1_ref, own_ref, other_ref):
    nv, lead, q = come0_ref.shape
    _, ob, half, _ = own_ref.shape
    slab = 2 * half
    n = nv * slab
    first = at_ref[0] == 0
    blocks = [come0_ref[:, :slab], come1_ref[...]]
    if lead > slab:
        blocks[1] = jnp.concatenate([come0_ref[:, slab:], blocks[1]], axis=1)
    for k, block in enumerate(blocks):
        cols = block.reshape(n, q)
        for i in range(ob):
            rows = mine_ref[:, i * slab : (i + 1) * slab].reshape(n, q)
            out = lax.dot_general(rows, cols, (((1,), (1,)), ((), ())), preferred_element_type=F32)
            out = out.reshape(nv, 2, half, n)
            own_ref[:, i, :, k * n : (k + 1) * n] = jnp.where(first, out[:, 0], out[:, 1])
            other_ref[:, i, :, k * n : (k + 1) * n] = jnp.where(first, out[:, 1], out[:, 0]).astype(BF)


def product(at, mine, come0, come1, ob, slab):
    nv = mine.shape[0]
    shape = (nv, ob, slab // 2, ob * nv * slab)
    return pl.pallas_call(
        product_kernel,
        out_shape=[jax.ShapeDtypeStruct(shape, F32), jax.ShapeDtypeStruct(shape, BF)],
        in_specs=[SMEM, VMEM, VMEM, VMEM],
        out_specs=[VMEM, VMEM],
        compiler_params=vmem(24),
    )(at, mine, come0, come1)


def core_sum_kernel(own_ref, other_ref, o_ref):
    o_ref[...] = (own_ref[...] + other_ref[...].astype(F32)).astype(BF)


def core_sum(own, other):
    nv, ob, half, cols = own.shape
    spec = pl.BlockSpec((2, ob, half, cols), lambda r: (r, 0, 0, 0))
    return pl.pallas_call(
        core_sum_kernel,
        grid=(nv // 2,),
        out_shape=jax.ShapeDtypeStruct(own.shape, BF),
        in_specs=[spec, spec],
        out_specs=spec,
        compiler_params=vmem(8),
    )(own, other)


def gather_sum_kernel(p0_ref, p1_ref, keep_ref, turn_ref):
    rows = []
    for k, ref in enumerate((p0_ref, p1_ref)):
        total = ref[0].astype(F32)
        for src in range(1, ref.shape[0]):
            total += ref[src].astype(F32)
        keep_ref[:, k] = total
        rows.append(total.reshape(-1, total.shape[2]))
    turned = jnp.concatenate(rows, axis=0).T
    turn_ref[...] = turned.reshape(turn_ref.shape).astype(BF)


def gather_sum(parts):
    ranks, ob, half, cols = parts.shape
    nvir, lanes = cols // ob, 2 * ob * half
    steps = nvir // lanes
    return pl.pallas_call(
        gather_sum_kernel,
        grid=(steps,),
        out_shape=[
            jax.ShapeDtypeStruct((ob, ob, half, nvir), F32),
            jax.ShapeDtypeStruct((nvir // half, half, lanes), BF),
        ],
        in_specs=[
            pl.BlockSpec((ranks, ob, half, lanes), lambda j: (0, 0, 0, j)),
            pl.BlockSpec((ranks, ob, half, lanes), lambda j: (0, 0, 0, j + steps)),
        ],
        out_specs=[
            pl.BlockSpec((ob, ob, half, lanes), lambda j: (0, 0, 0, j)),
            pl.BlockSpec((lanes // half, half, lanes), lambda j: (j, 0, 0)),
        ],
        compiler_params=vmem(8),
    )(parts, parts)


def density_kernel(e_ref, slot_ref, keep_ref, turn_ref, vc_ref, vall_ref, o_ref):
    ob, _, half, nvir = keep_ref.shape
    ranks, _, lanes = turn_ref.shape
    nv = ranks // 2
    spots = lanes // half
    spot = lax.broadcasted_iota(jnp.int32, (half, lanes), 1) // half
    turned = {}
    for g in range(ranks // spots):
        moved = []
        for j in range(spots):
            x = turn_ref[g * spots + j].astype(F32)
            moved.append([x] + [pltpu.roll(x, n * half, 1) for n in range(1, spots)])
        for ki in range(spots):
            whole = moved[0][(-ki) % spots]
            for j in range(1, spots):
                whole = jnp.where(spot == j, moved[j][(j - ki) % spots], whole)
            turned.setdefault((ki % ob, ki // ob), []).append(whole)
    turned = {ik: jnp.concatenate(x, axis=1) for ik, x in turned.items()}

    def swap(x):
        return pltpu.roll(x, lanes // 2, 1)

    t1, c1, t2, c2 = {}, {}, {}, {}
    for i in range(ob):
        for k in range(ob):
            x1 = keep_ref[i, k]
            x2 = turned[i, k]
            denom = (e_ref[i] + e_ref[ob + k]) - vc_ref[...] - vall_ref[...]
            t1[i, k] = (x1 / denom).astype(BF)
            t2[i, k] = (x2 / denom).astype(BF)
            c1[i, k] = ((2.0 * x1 - x2) / denom).astype(BF)
            c2[i, k] = ((2.0 * x2 - x1) / denom).astype(BF)
    order = [(i, k) for i in range(ob) for k in range(ob)]
    amps = jnp.concatenate([t1[x] for x in order] + [t2[x] for x in order], axis=0)
    contra = jnp.concatenate([c1[x] for x in order] + [c2[x] for x in order], axis=0)
    vt = lax.dot_general(contra, amps, (((0,), (0,)), ((), ())), preferred_element_type=F32)
    split = vt.reshape(nvir // 16, 2, 8, nvir)
    h0 = split[:, 0].reshape(nvir // 2, nvir)
    h1 = split[:, 1].reshape(nvir // 2, nvir)
    low = lax.broadcasted_iota(jnp.int32, (nvir // 2, lanes), 1) < lanes // 2
    planes = (o_ref.shape[1] - 16) // 8
    for j in range(nv // 2):
        x, y = h0[:, j * lanes : (j + 1) * lanes], h1[:, j * lanes : (j + 1) * lanes]
        for n, piece in enumerate((jnp.where(low, x, swap(y)), jnp.where(low, swap(x), y))):
            piece = piece.reshape(2, planes, 2, 8, lanes)
            for slot in range(4):
                rows = piece[slot // 2, :, slot % 2].reshape(8 * planes, lanes)
                o_ref[slot * nv + 2 * j + n, : 8 * planes] = rows.astype(o_ref.dtype)

    def dot(x, y):
        rows = jnp.sum(x.astype(F32) * y.astype(F32), axis=0, keepdims=True)
        return sum(rows[:, j * lanes : (j + 1) * lanes] for j in range(nvir // lanes))

    occ = [-sum(dot(t1[i, k], c1[m, k]) for k in range(ob)) for i in range(ob) for m in range(ob)]
    occ += [-sum(dot(t2[i, k], c2[i, n]) for i in range(ob)) for k in range(ob) for n in range(ob)]
    occ = jnp.concatenate(occ, axis=0)
    stays = lax.broadcasted_iota(jnp.int32, occ.shape, 0) < ob * ob
    goes_to = jnp.where(stays, slot_ref[0], slot_ref[1])
    for slot in range(4):
        mine = jnp.where(goes_to == slot, occ, 0.0)
        high = mine.astype(BF)
        rest = (mine - high.astype(F32)).astype(BF)
        tail = jnp.concatenate([high, rest], axis=0)
        for v in range(nv):
            o_ref[slot * nv + v, 8 * planes :] = tail


def density(energies, slots, keep, turned, vc, vall, planes):
    ranks, _, lanes = turned.shape
    return pl.pallas_call(
        density_kernel,
        out_shape=jax.ShapeDtypeStruct((2 * ranks, 8 * planes + 16, lanes), BF),
        in_specs=[SMEM, SMEM] + [VMEM] * 4,
        out_specs=VMEM,
        compiler_params=vmem(16),
    )(energies, slots, keep, turned, vc, vall)


def plane_sum_kernel(at_ref, p_ref, o_ref):
    total = p_ref[0].astype(F32)
    for src in range(1, p_ref.shape[0]):
        total += p_ref[src].astype(F32)
    planes = o_ref.shape[0]
    n = 8 * planes
    occ = total[n : n + 8] + total[n + 8 : n + 16]
    other = pltpu.roll(occ, 4, 0)
    for z in range(planes):
        o_ref[z, :8] = total[8 * z : 8 * z + 8]
        o_ref[z, 8:] = jnp.where(at_ref[0] == z, occ, 0.0) + jnp.where(at_ref[1] == z, other, 0.0)


def plane_sum(at, parts, planes):
    return pl.pallas_call(
        plane_sum_kernel,
        out_shape=jax.ShapeDtypeStruct((planes, 16, parts.shape[2]), F32),
        in_specs=[SMEM, VMEM],
        out_specs=VMEM,
        compiler_params=vmem(8),
    )(at, parts)


def last_sum_kernel(p_ref, occ_ref, vir_ref):
    total = p_ref[0]
    for src in range(1, p_ref.shape[0]):
        total += p_ref[src]
    slab = vir_ref.shape[1]
    vir_ref[:8] = total[:8, :slab]
    vir_ref[8:] = total[:8, slab:]
    occ = jnp.sum(total[8:], axis=1, keepdims=True)
    ob = occ_ref.shape[0]
    for i in range(ob):
        for m in range(ob):
            occ_ref[i : i + 1, m : m + 1] = occ[ob * i + m : ob * i + m + 1]


def last_sum(parts, ob, slab):
    return pl.pallas_call(
        last_sum_kernel,
        out_shape=[
            jax.ShapeDtypeStruct((ob, ob), F32),
            jax.ShapeDtypeStruct((16, slab), F32),
        ],
        in_specs=[VMEM],
        out_specs=[VMEM, VMEM],
        compiler_params=vmem(4),
    )(parts)


def chip_groups(count, lanes):
    return [
        [(low + core) * lanes + v for v in range(lanes) for core in range(2)]
        for low in range(0, count, 2)
    ]


def plane_groups(count, lanes):
    planes = count // 4
    return [
        [((y * planes + z) * 2 + core) * lanes + v for y in range(2) for core in range(2) for v in range(lanes)]
        for z in range(planes)
    ]


def column_groups(count):
    planes = count // 4
    return [[(y * planes + z) * 2 + core for z in range(planes)] for y in range(2) for core in range(2)]


def by_chip(offset, count, branch, *operands):
    return lax.switch(offset, [functools.partial(branch, m) for m in range(count // 2)], *operands)


def per_device(three_index, occ_energy, vir_energy, partner):
    ob, slab, naux = three_index.shape
    nvir = vir_energy.shape[0]
    count, lanes = lax.axis_size("occ"), lax.axis_size("vir")
    p, v = lax.axis_index("occ"), lax.axis_index("vir")
    offset = jnp.bitwise_xor(p, partner[0])
    chip, core = p // 2, p % 2
    far, cross = offset // 2, offset % 2
    higher = chip > jnp.bitwise_xor(chip, far)
    stay_core = jnp.where(higher, 1 - cross, 0)
    stay = 2 * chip + stay_core
    come = jnp.bitwise_xor(stay, offset)
    half = slab // 2
    groups = chip_groups(count, lanes)

    def over_vir(x):
        return lax.all_to_all(x, "vir", 0, 0, tiled=True)

    def over_chips(x):
        return lax.all_to_all(x, BOTH, 0, 0, axis_index_groups=groups, tiled=True)

    def to_chip(m, x, turn=0):
        route = [
            (a * lanes + w, (a ^ 2 * m) * lanes + (w ^ turn)) for a in range(count) for w in range(lanes)
        ]
        return lax.ppermute(x, BOTH, route) if m else x

    def to_sibling(x):
        return lax.ppermute(x, "occ", [(a, a ^ 1) for a in range(count)])

    row = lanes // 2
    upper = v // row

    def by_half(m):
        return m // (count // 4) == 1 and m % (count // 4) < 2

    def lead_on(m, x):
        if not by_half(m):
            return (to_chip(m, x),)
        stay = lax.dynamic_slice_in_dim(x, upper * row, row)
        turn = lax.dynamic_slice_in_dim(x, (1 - upper) * row, row)
        return to_chip(m, stay), to_chip(m, turn, row)

    def lead_over(m, straight, *turned):
        if not turned:
            return over_vir(straight)
        (turned,) = turned
        flip = upper == 1
        both = jnp.stack(
            [jnp.where(flip, turned, straight), jnp.where(flip, straight, turned)], axis=1
        )
        halves = [list(range(row)), list(range(row, lanes))]
        both = lax.all_to_all(both, "vir", 0, 0, axis_index_groups=halves, tiled=True)
        return jnp.swapaxes(both, 0, 1).reshape((lanes,) + both.shape[2:])

    def exchange(m, at, x, other0, other1, lead):
        def step(run, *operands):
            like = jax.eval_shape(run, *operands)
            never = lambda *_: jax.tree.map(lambda y: jnp.zeros(y.shape, y.dtype), like)
            return lax.cond(partner[0] >= 0, run, never, *operands)

        def spread(*operands):
            mine = over_vir(pick(*operands))
            return mine, mine[:, ob * slab :]

        lead = lead_on(m, lead)
        mine, last = step(spread, at, x, other0, other1)
        if by_half(m):
            lead, last = lax.optimization_barrier((lead, last))
        last = to_chip(m, last)
        lead, mine = lax.optimization_barrier((lead, mine))
        return mine, step(functools.partial(lead_over, m), *lead), last

    lead_rows = slab + slab // 4
    last_rows = ob * slab - lead_rows
    at = jnp.stack([core, (core == stay_core).astype(jnp.int32)])
    their0, their1, lead = cut(at, three_index, lanes, lead_rows)
    other0, other1 = to_sibling(their0), to_sibling(their1)
    lead = jnp.where(core == stay_core, other0, lead)
    mine, come0, come1 = by_chip(far, count, exchange, at, three_index, other0, other1, lead)
    own, others = product(at, mine, come0, come1, ob, slab)
    keep, turn = gather_sum(over_vir(core_sum(own, to_sibling(others))))
    turned = over_chips(turn)
    energies = jnp.concatenate([
        lax.dynamic_slice_in_dim(occ_energy, stay * ob, ob),
        lax.dynamic_slice_in_dim(occ_energy, come * ob, ob),
    ])
    vc = lax.dynamic_slice_in_dim(vir_energy, v * slab + core * half, half)
    planes = count // 4

    def slot_of(block):
        return block // (2 * planes) * 2 + block % 2

    def plane_of(block):
        return block // 2 % planes

    packed = density(
        energies, jnp.stack([slot_of(stay), slot_of(come)]), keep, turned,
        vc.reshape(half, 1), vir_energy.reshape(1, nvir), planes,
    )
    parts = lax.all_to_all(
        packed, BOTH, 0, 0, axis_index_groups=plane_groups(count, lanes), tiled=True
    )
    pieces = plane_sum(jnp.stack([plane_of(stay), plane_of(come)]), parts, planes)
    parts = lax.all_to_all(
        pieces, "occ", 0, 0, axis_index_groups=column_groups(count), tiled=True
    )
    occ_density, vir_turned = last_sum(parts, ob, slab)
    return occ_density, vir_turned.T


def solution(mesh):
    in_specs = (P("occ", "vir", None), P(), P(), P("occ"))
    out_specs = (P("occ", None), P("vir", "occ"))
    return jax.shard_map(
        per_device, mesh=mesh, in_specs=in_specs, out_specs=out_specs, check_vma=False
    )
```

```python
import functools

import jax
import jax.numpy as jnp
from jax import lax
from jax.experimental import pallas as pl
from jax.experimental.pallas import tpu as pltpu
from jax.sharding import PartitionSpec as P

BF = jnp.bfloat16
F32 = jnp.float32
BOTH = ("occ", "vir")
SMEM = pl.BlockSpec(memory_space=pltpu.SMEM)
VMEM = pl.BlockSpec(memory_space=pltpu.VMEM)
ANY = pl.BlockSpec(memory_space=pl.ANY)
HBM = pl.BlockSpec(memory_space=pltpu.HBM)


def vmem(mib):
    return pltpu.CompilerParams(vmem_limit_bytes=mib * 1024 * 1024)


def copy_all(parts, copies_of, sems):
    def each(w, begin):
        for n, (src, dst) in enumerate(copies_of(w)):
            copy = pltpu.make_async_copy(src, dst, sems.at[w, n])
            copy.start() if begin else copy.wait()

    lax.fori_loop(0, parts, lambda w, _: each(w, True), None)
    lax.fori_loop(0, parts, lambda w, _: each(w, False), None)


def cut_kernel(at_ref, x_ref, their0_ref, their1_ref, own_ref, sems):
    parts, lead, q = own_ref.shape
    slab = x_ref.shape[1]
    more = lead - slab

    def copies_of(w):
        theirs = pl.ds(pl.multiple_of(((1 - at_ref[0]) * parts + w) * q, q), q)
        mine = pl.ds(pl.multiple_of((at_ref[0] * parts + w) * q, q), q)
        copies = [
            (x_ref.at[0, :, theirs], their0_ref.at[w, :slab]),
            (x_ref.at[1, more:, theirs], their1_ref.at[w]),
            (x_ref.at[0, :, mine], own_ref.at[w, :slab]),
        ]
        if more:
            copies += [
                (x_ref.at[1, :more, theirs], their0_ref.at[w, slab:]),
                (x_ref.at[1, :more, mine], own_ref.at[w, slab:]),
            ]
        return copies

    copy_all(parts, copies_of, sems)


def cut(at, x, parts, lead):
    ob, slab, naux = x.shape
    q = naux // (2 * parts)
    return pl.pallas_call(
        cut_kernel,
        out_shape=[
            jax.ShapeDtypeStruct((parts, rows, q), x.dtype)
            for rows in (lead, ob * slab - lead, lead)
        ],
        in_specs=[SMEM, HBM],
        out_specs=[VMEM] * 3,
        scratch_shapes=[pltpu.SemaphoreType.DMA((parts, 5))],
        compiler_params=vmem(8),
    )(at, x)


def pick_kernel(at_ref, x_ref, other0_ref, other1_ref, o_ref, sems):
    parts, rows, q = o_ref.shape
    lead, last = other0_ref.shape[1], other1_ref.shape[1]
    slab = x_ref.shape[1]
    more = lead - slab

    def fill(stays):
        def copies_of(w):
            mine = pl.ds(pl.multiple_of((at_ref[0] * parts + w) * q, q), q)
            if stays:
                return [
                    (x_ref.at[0, :, mine], o_ref.at[w, :slab]),
                    (x_ref.at[1, :, mine], o_ref.at[w, slab : 2 * slab]),
                    (other1_ref.at[w], o_ref.at[w, 2 * slab :]),
                ]
            return [
                (other0_ref.at[w], o_ref.at[w, :lead]),
                (other1_ref.at[w], o_ref.at[w, lead : lead + last]),
                (x_ref.at[1, more:, mine], o_ref.at[w, 2 * slab :]),
            ]

        copy_all(parts, copies_of, sems)

    pl.when(at_ref[1] != 0)(lambda: fill(True))
    pl.when(at_ref[1] == 0)(lambda: fill(False))


def pick(at, x, other0, other1):
    parts, lead, q = other0.shape
    last = other1.shape[1]
    return pl.pallas_call(
        pick_kernel,
        out_shape=jax.ShapeDtypeStruct((parts, lead + 2 * last, q), x.dtype),
        in_specs=[SMEM, HBM, ANY, ANY],
        out_specs=VMEM,
        scratch_shapes=[pltpu.SemaphoreType.DMA((parts, 3))],
        compiler_params=vmem(8),
    )(at, x, other0, other1)


def product_kernel(own, at_ref, mine_ref, come0_ref, come1_ref, o_ref):
    nv, lead, q = come0_ref.shape
    half = o_ref.shape[2]
    slab = 2 * half
    n = nv * slab
    core = at_ref[0] if own else 1 - at_ref[0]
    blocks = [come0_ref[:, :slab], come1_ref[...]]
    if lead > slab:
        blocks[1] = jnp.concatenate([come0_ref[:, slab:], blocks[1]], axis=1)
    start = pl.multiple_of(core * half, half)
    rows = mine_ref[:, pl.ds(start, half)].reshape(nv * half, q)
    for k, block in enumerate(blocks):
        out = lax.dot_general(
            rows, block.reshape(n, q), (((1,), (1,)), ((), ())), preferred_element_type=F32
        )
        o_ref[:, 0, :, k * n : (k + 1) * n] = out.reshape(nv, half, n).astype(o_ref.dtype)


def product(own, at, mine, come0, come1, ob, slab):
    nv, _, q = mine.shape
    cols = ob * nv * slab
    return pl.pallas_call(
        functools.partial(product_kernel, own),
        grid=(ob,),
        out_shape=jax.ShapeDtypeStruct((nv, ob, slab // 2, cols), F32 if own else BF),
        in_specs=[
            SMEM,
            pl.BlockSpec((nv, slab, q), lambda i: (0, i, 0)),
            pl.BlockSpec(come0.shape, lambda i: (0, 0, 0)),
            pl.BlockSpec(come1.shape, lambda i: (0, 0, 0)),
        ],
        out_specs=pl.BlockSpec((nv, 1, slab // 2, cols), lambda i: (0, i, 0, 0)),
        compiler_params=vmem(24),
    )(at, mine, come0, come1)


def core_sum_kernel(own_ref, other_ref, o_ref):
    o_ref[...] = (own_ref[...] + other_ref[...].astype(F32)).astype(BF)


def core_sum(own, other):
    nv, ob, half, cols = own.shape
    spec = pl.BlockSpec((4, ob, half, cols), lambda r: (r, 0, 0, 0))
    return pl.pallas_call(
        core_sum_kernel,
        grid=(nv // 4,),
        out_shape=jax.ShapeDtypeStruct(own.shape, BF),
        in_specs=[spec, spec],
        out_specs=spec,
        compiler_params=vmem(8),
    )(own, other)


def gather_sum_kernel(p0_ref, p1_ref, keep_ref, turn_ref):
    rows = []
    for k, ref in enumerate((p0_ref, p1_ref)):
        total = ref[0].astype(F32)
        for src in range(1, ref.shape[0]):
            total += ref[src].astype(F32)
        keep_ref[:, k] = total
        rows.append(total.reshape(-1, total.shape[2]))
    turned = jnp.concatenate(rows, axis=0).T
    turn_ref[...] = turned.reshape(turn_ref.shape).astype(BF)


def gather_sum(parts):
    ranks, ob, half, cols = parts.shape
    nvir, lanes = cols // ob, 2 * ob * half
    steps = nvir // lanes
    return pl.pallas_call(
        gather_sum_kernel,
        grid=(steps,),
        out_shape=[
            jax.ShapeDtypeStruct((ob, ob, half, nvir), F32),
            jax.ShapeDtypeStruct((nvir // half, half, lanes), BF),
        ],
        in_specs=[
            pl.BlockSpec((ranks, ob, half, lanes), lambda j: (0, 0, 0, j)),
            pl.BlockSpec((ranks, ob, half, lanes), lambda j: (0, 0, 0, j + steps)),
        ],
        out_specs=[
            pl.BlockSpec((ob, ob, half, lanes), lambda j: (0, 0, 0, j)),
            pl.BlockSpec((lanes // half, half, lanes), lambda j: (j, 0, 0)),
        ],
        compiler_params=vmem(8),
    )(parts, parts)


def density_kernel(e_ref, slot_ref, keep_ref, turn_ref, vc_ref, vall_ref, o_ref):
    ob, _, half, nvir = keep_ref.shape
    ranks, _, lanes = turn_ref.shape
    nv = ranks // 2
    spots = lanes // half
    spot = lax.broadcasted_iota(jnp.int32, (half, lanes), 1) // half
    turned = {}
    for g in range(ranks // spots):
        moved = []
        for j in range(spots):
            x = turn_ref[g * spots + j].astype(F32)
            moved.append([x] + [pltpu.roll(x, n * half, 1) for n in range(1, spots)])
        for ki in range(spots):
            whole = moved[0][(-ki) % spots]
            for j in range(1, spots):
                whole = jnp.where(spot == j, moved[j][(j - ki) % spots], whole)
            turned.setdefault((ki % ob, ki // ob), []).append(whole)
    turned = {ik: jnp.concatenate(x, axis=1) for ik, x in turned.items()}

    def swap(x):
        return pltpu.roll(x, lanes // 2, 1)

    t1, c1, t2, c2 = {}, {}, {}, {}
    for i in range(ob):
        for k in range(ob):
            x1 = keep_ref[i, k]
            x2 = turned[i, k]
            denom = (e_ref[i] + e_ref[ob + k]) - vc_ref[...] - vall_ref[...]
            t1[i, k] = (x1 / denom).astype(BF)
            t2[i, k] = (x2 / denom).astype(BF)
            c1[i, k] = ((2.0 * x1 - x2) / denom).astype(BF)
            c2[i, k] = ((2.0 * x2 - x1) / denom).astype(BF)
    order = [(i, k) for i in range(ob) for k in range(ob)]
    amps = jnp.concatenate([t1[x] for x in order] + [t2[x] for x in order], axis=0)
    contra = jnp.concatenate([c1[x] for x in order] + [c2[x] for x in order], axis=0)
    vt = lax.dot_general(contra, amps, (((0,), (0,)), ((), ())), preferred_element_type=F32)
    split = vt.reshape(nvir // 16, 2, 8, nvir)
    h0 = split[:, 0].reshape(nvir // 2, nvir)
    h1 = split[:, 1].reshape(nvir // 2, nvir)
    low = lax.broadcasted_iota(jnp.int32, (nvir // 2, lanes), 1) < lanes // 2
    planes = (o_ref.shape[1] - 16) // 8
    for j in range(nv // 2):
        x, y = h0[:, j * lanes : (j + 1) * lanes], h1[:, j * lanes : (j + 1) * lanes]
        for n, piece in enumerate((jnp.where(low, x, swap(y)), jnp.where(low, swap(x), y))):
            piece = piece.reshape(2, planes, 2, 8, lanes)
            for slot in range(4):
                rows = piece[slot // 2, :, slot % 2].reshape(8 * planes, lanes)
                o_ref[slot * nv + 2 * j + n, : 8 * planes] = rows.astype(o_ref.dtype)

    def dot(x, y):
        rows = jnp.sum(x.astype(F32) * y.astype(F32), axis=0, keepdims=True)
        return sum(rows[:, j * lanes : (j + 1) * lanes] for j in range(nvir // lanes))

    occ = [-sum(dot(t1[i, k], c1[m, k]) for k in range(ob)) for i in range(ob) for m in range(ob)]
    occ += [-sum(dot(t2[i, k], c2[i, n]) for i in range(ob)) for k in range(ob) for n in range(ob)]
    occ = jnp.concatenate(occ, axis=0)
    stays = lax.broadcasted_iota(jnp.int32, occ.shape, 0) < ob * ob
    goes_to = jnp.where(stays, slot_ref[0], slot_ref[1])
    for slot in range(4):
        mine = jnp.where(goes_to == slot, occ, 0.0)
        high = mine.astype(BF)
        rest = (mine - high.astype(F32)).astype(BF)
        tail = jnp.concatenate([high, rest], axis=0)
        for v in range(nv):
            o_ref[slot * nv + v, 8 * planes :] = tail


def density(energies, slots, keep, turned, vc, vall, planes):
    ranks, _, lanes = turned.shape
    return pl.pallas_call(
        density_kernel,
        out_shape=jax.ShapeDtypeStruct((2 * ranks, 8 * planes + 16, lanes), BF),
        in_specs=[SMEM, SMEM] + [VMEM] * 4,
        out_specs=VMEM,
        compiler_params=vmem(16),
    )(energies, slots, keep, turned, vc, vall)


def plane_sum_kernel(at_ref, p_ref, o_ref):
    total = p_ref[0].astype(F32)
    for src in range(1, p_ref.shape[0]):
        total += p_ref[src].astype(F32)
    planes = o_ref.shape[0]
    n = 8 * planes
    occ = total[n : n + 8] + total[n + 8 : n + 16]
    other = pltpu.roll(occ, 4, 0)
    for z in range(planes):
        o_ref[z, :8] = total[8 * z : 8 * z + 8]
        o_ref[z, 8:] = jnp.where(at_ref[0] == z, occ, 0.0) + jnp.where(at_ref[1] == z, other, 0.0)


def plane_sum(at, parts, planes):
    return pl.pallas_call(
        plane_sum_kernel,
        out_shape=jax.ShapeDtypeStruct((planes, 16, parts.shape[2]), F32),
        in_specs=[SMEM, VMEM],
        out_specs=VMEM,
        compiler_params=vmem(8),
    )(at, parts)


def last_sum_kernel(p_ref, occ_ref, vir_ref):
    total = p_ref[0]
    for src in range(1, p_ref.shape[0]):
        total += p_ref[src]
    slab = vir_ref.shape[1]
    vir_ref[:8] = total[:8, :slab]
    vir_ref[8:] = total[:8, slab:]
    occ = jnp.sum(total[8:], axis=1, keepdims=True)
    ob = occ_ref.shape[0]
    for i in range(ob):
        for m in range(ob):
            occ_ref[i : i + 1, m : m + 1] = occ[ob * i + m : ob * i + m + 1]


def last_sum(parts, ob, slab):
    return pl.pallas_call(
        last_sum_kernel,
        out_shape=[
            jax.ShapeDtypeStruct((ob, ob), F32),
            jax.ShapeDtypeStruct((16, slab), F32),
        ],
        in_specs=[VMEM],
        out_specs=[VMEM, VMEM],
        compiler_params=vmem(4),
    )(parts)


def chip_groups(count, lanes):
    return [
        [(low + core) * lanes + v for v in range(lanes) for core in range(2)]
        for low in range(0, count, 2)
    ]


def plane_groups(count, lanes):
    planes = count // 4
    return [
        [((y * planes + z) * 2 + core) * lanes + v for y in range(2) for core in range(2) for v in range(lanes)]
        for z in range(planes)
    ]


def column_groups(count):
    planes = count // 4
    return [[(y * planes + z) * 2 + core for z in range(planes)] for y in range(2) for core in range(2)]


def by_chip(offset, count, branch, *operands):
    return lax.switch(offset, [functools.partial(branch, m) for m in range(count // 2)], *operands)


def per_device(three_index, occ_energy, vir_energy, partner):
    ob, slab, naux = three_index.shape
    nvir = vir_energy.shape[0]
    count, lanes = lax.axis_size("occ"), lax.axis_size("vir")
    p, v = lax.axis_index("occ"), lax.axis_index("vir")
    offset = jnp.bitwise_xor(p, partner[0])
    chip, core = p // 2, p % 2
    far, cross = offset // 2, offset % 2
    higher = chip > jnp.bitwise_xor(chip, far)
    stay_core = jnp.where(higher, 1 - cross, 0)
    stay = 2 * chip + stay_core
    come = jnp.bitwise_xor(stay, offset)
    half = slab // 2
    groups = chip_groups(count, lanes)

    def over_vir(x):
        return lax.all_to_all(x, "vir", 0, 0, tiled=True)

    def over_chips(x):
        return lax.all_to_all(x, BOTH, 0, 0, axis_index_groups=groups, tiled=True)

    def to_chip(m, x, turn=0):
        route = [
            (a * lanes + w, (a ^ 2 * m) * lanes + (w ^ turn)) for a in range(count) for w in range(lanes)
        ]
        return lax.ppermute(x, BOTH, route) if m else x

    def to_sibling(x):
        return lax.ppermute(x, "occ", [(a, a ^ 1) for a in range(count)])

    row = lanes // 2
    upper = v // row

    def by_half(m):
        return m // (count // 4) == 1 and m % (count // 4) < 2

    def lead_on(m, x):
        if not by_half(m):
            return (to_chip(m, x),)
        stay = lax.dynamic_slice_in_dim(x, upper * row, row)
        turn = lax.dynamic_slice_in_dim(x, (1 - upper) * row, row)
        return to_chip(m, stay), to_chip(m, turn, row)

    def lead_over(m, straight, *turned):
        if not turned:
            return over_vir(straight)
        (turned,) = turned
        flip = upper == 1
        both = jnp.stack(
            [jnp.where(flip, turned, straight), jnp.where(flip, straight, turned)], axis=1
        )
        halves = [list(range(row)), list(range(row, lanes))]
        both = lax.all_to_all(both, "vir", 0, 0, axis_index_groups=halves, tiled=True)
        return jnp.swapaxes(both, 0, 1).reshape((lanes,) + both.shape[2:])

    def exchange(m, at, x, other0, other1, lead):
        def step(run, *operands):
            like = jax.eval_shape(run, *operands)
            never = lambda *_: jax.tree.map(lambda y: jnp.zeros(y.shape, y.dtype), like)
            return lax.cond(partner[0] >= 0, run, never, *operands)

        def spread(*operands):
            mine = over_vir(pick(*operands))
            return mine, mine[:, ob * slab :]

        lead = lead_on(m, lead)
        mine, last = step(spread, at, x, other0, other1)
        if by_half(m):
            lead, last = lax.optimization_barrier((lead, last))
        last = to_chip(m, last)
        lead, mine = lax.optimization_barrier((lead, mine))
        return mine, step(functools.partial(lead_over, m), *lead), last

    lead_rows = slab + slab // 4
    last_rows = ob * slab - lead_rows
    at = jnp.stack([core, (core == stay_core).astype(jnp.int32)])
    their0, their1, lead = cut(at, three_index, lanes, lead_rows)
    other0, other1 = to_sibling(their0), to_sibling(their1)
    lead = jnp.where(core == stay_core, other0, lead)
    mine, come0, come1 = by_chip(far, count, exchange, at, three_index, other0, other1, lead)
    others = to_sibling(product(False, at, mine, come0, come1, ob, slab))
    own = product(True, at, mine, come0, come1, ob, slab)
    keep, turn = gather_sum(over_vir(core_sum(own, others)))
    turned = over_chips(turn)
    energies = jnp.concatenate([
        lax.dynamic_slice_in_dim(occ_energy, stay * ob, ob),
        lax.dynamic_slice_in_dim(occ_energy, come * ob, ob),
    ])
    vc = lax.dynamic_slice_in_dim(vir_energy, v * slab + core * half, half)
    planes = count // 4

    def slot_of(block):
        return block // (2 * planes) * 2 + block % 2

    def plane_of(block):
        return block // 2 % planes

    packed = density(
        energies, jnp.stack([slot_of(stay), slot_of(come)]), keep, turned,
        vc.reshape(half, 1), vir_energy.reshape(1, nvir), planes,
    )
    parts = lax.all_to_all(
        packed, BOTH, 0, 0, axis_index_groups=plane_groups(count, lanes), tiled=True
    )
    pieces = plane_sum(jnp.stack([plane_of(stay), plane_of(come)]), parts, planes)
    parts = lax.all_to_all(
        pieces, "occ", 0, 0, axis_index_groups=column_groups(count), tiled=True
    )
    occ_density, vir_turned = last_sum(parts, ob, slab)
    return occ_density, vir_turned.T


def solution(mesh):
    in_specs = (P("occ", "vir", None), P(), P(), P("occ"))
    out_specs = (P("occ", None), P("vir", "occ"))
    return jax.shard_map(
        per_device, mesh=mesh, in_specs=in_specs, out_specs=out_specs, check_vma=False
    )
```

```python
import functools

import jax
import jax.numpy as jnp
from jax import lax
from jax.experimental import pallas as pl
from jax.experimental.pallas import tpu as pltpu
from jax.sharding import PartitionSpec as P

BF = jnp.bfloat16
F32 = jnp.float32
BOTH = ("occ", "vir")
SMEM = pl.BlockSpec(memory_space=pltpu.SMEM)
VMEM = pl.BlockSpec(memory_space=pltpu.VMEM)
ANY = pl.BlockSpec(memory_space=pl.ANY)
HBM = pl.BlockSpec(memory_space=pltpu.HBM)


def vmem(mib):
    return pltpu.CompilerParams(vmem_limit_bytes=mib * 1024 * 1024)


def copy_all(parts, copies_of, sems):
    def each(w, begin):
        for n, (src, dst) in enumerate(copies_of(w)):
            copy = pltpu.make_async_copy(src, dst, sems.at[w, n])
            copy.start() if begin else copy.wait()

    lax.fori_loop(0, parts, lambda w, _: each(w, True), None)
    lax.fori_loop(0, parts, lambda w, _: each(w, False), None)


def cut_kernel(at_ref, x_ref, their0_ref, their1_ref, own_ref, sems):
    parts, lead, q = own_ref.shape
    slab = x_ref.shape[1]
    more = lead - slab

    def copies_of(w):
        theirs = pl.ds(pl.multiple_of(((1 - at_ref[0]) * parts + w) * q, q), q)
        mine = pl.ds(pl.multiple_of((at_ref[0] * parts + w) * q, q), q)
        copies = [
            (x_ref.at[0, :, theirs], their0_ref.at[w, :slab]),
            (x_ref.at[1, more:, theirs], their1_ref.at[w]),
            (x_ref.at[0, :, mine], own_ref.at[w, :slab]),
        ]
        if more:
            copies += [
                (x_ref.at[1, :more, theirs], their0_ref.at[w, slab:]),
                (x_ref.at[1, :more, mine], own_ref.at[w, slab:]),
            ]
        return copies

    copy_all(parts, copies_of, sems)


def cut(at, x, parts, lead):
    ob, slab, naux = x.shape
    q = naux // (2 * parts)
    return pl.pallas_call(
        cut_kernel,
        out_shape=[
            jax.ShapeDtypeStruct((parts, rows, q), x.dtype)
            for rows in (lead, ob * slab - lead, lead)
        ],
        in_specs=[SMEM, HBM],
        out_specs=[VMEM] * 3,
        scratch_shapes=[pltpu.SemaphoreType.DMA((parts, 5))],
        compiler_params=vmem(8),
    )(at, x)


def pick_kernel(at_ref, x_ref, other0_ref, other1_ref, o_ref, sems):
    parts, rows, q = o_ref.shape
    lead, last = other0_ref.shape[1], other1_ref.shape[1]
    slab = x_ref.shape[1]
    more = lead - slab

    def fill(stays):
        def copies_of(w):
            mine = pl.ds(pl.multiple_of((at_ref[0] * parts + w) * q, q), q)
            if stays:
                return [
                    (x_ref.at[0, :, mine], o_ref.at[w, :slab]),
                    (x_ref.at[1, :, mine], o_ref.at[w, slab : 2 * slab]),
                    (other1_ref.at[w], o_ref.at[w, 2 * slab :]),
                ]
            return [
                (other0_ref.at[w], o_ref.at[w, :lead]),
                (other1_ref.at[w], o_ref.at[w, lead : lead + last]),
                (x_ref.at[1, more:, mine], o_ref.at[w, 2 * slab :]),
            ]

        copy_all(parts, copies_of, sems)

    pl.when(at_ref[1] != 0)(lambda: fill(True))
    pl.when(at_ref[1] == 0)(lambda: fill(False))


def pick(at, x, other0, other1):
    parts, lead, q = other0.shape
    last = other1.shape[1]
    return pl.pallas_call(
        pick_kernel,
        out_shape=jax.ShapeDtypeStruct((parts, lead + 2 * last, q), x.dtype),
        in_specs=[SMEM, HBM, ANY, ANY],
        out_specs=VMEM,
        scratch_shapes=[pltpu.SemaphoreType.DMA((parts, 3))],
        compiler_params=vmem(8),
    )(at, x, other0, other1)


def product_kernel(own, at_ref, mine_ref, come0_ref, come1_ref, o_ref):
    nv, lead, q = come0_ref.shape
    half = o_ref.shape[2]
    slab = 2 * half
    n = nv * slab
    core = at_ref[0] if own else 1 - at_ref[0]
    blocks = [come0_ref[:, :slab], come1_ref[...]]
    if lead > slab:
        blocks[1] = jnp.concatenate([come0_ref[:, slab:], blocks[1]], axis=1)
    start = pl.multiple_of(core * half, half)
    rows = mine_ref[:, pl.ds(start, half)].reshape(nv * half, q)
    for k, block in enumerate(blocks):
        out = lax.dot_general(
            rows, block.reshape(n, q), (((1,), (1,)), ((), ())), preferred_element_type=F32
        )
        o_ref[:, 0, :, k * n : (k + 1) * n] = out.reshape(nv, half, n).astype(o_ref.dtype)


def product(own, at, mine, come0, come1, ob, slab):
    nv, _, q = mine.shape
    cols = ob * nv * slab
    return pl.pallas_call(
        functools.partial(product_kernel, own),
        grid=(ob,),
        out_shape=jax.ShapeDtypeStruct((nv, ob, slab // 2, cols), F32 if own else BF),
        in_specs=[
            SMEM,
            pl.BlockSpec((nv, slab, q), lambda i: (0, i, 0)),
            pl.BlockSpec(come0.shape, lambda i: (0, 0, 0)),
            pl.BlockSpec(come1.shape, lambda i: (0, 0, 0)),
        ],
        out_specs=pl.BlockSpec((nv, 1, slab // 2, cols), lambda i: (0, i, 0, 0)),
        compiler_params=vmem(24),
    )(at, mine, come0, come1)


def core_sum_kernel(own_ref, other_ref, o_ref):
    o_ref[...] = (own_ref[...] + other_ref[...].astype(F32)).astype(BF)


def core_sum(own, other):
    nv, ob, half, cols = own.shape
    spec = pl.BlockSpec((4, ob, half, cols), lambda r: (r, 0, 0, 0))
    return pl.pallas_call(
        core_sum_kernel,
        grid=(nv // 4,),
        out_shape=jax.ShapeDtypeStruct(own.shape, BF),
        in_specs=[spec, spec],
        out_specs=spec,
        compiler_params=vmem(8),
    )(own, other)


def gather_sum_kernel(p0_ref, p1_ref, keep_ref, turn_ref):
    rows = []
    for k, ref in enumerate((p0_ref, p1_ref)):
        total = ref[0].astype(F32)
        for src in range(1, ref.shape[0]):
            total += ref[src].astype(F32)
        keep_ref[:, k] = total
        rows.append(total.reshape(-1, total.shape[2]))
    turned = jnp.concatenate(rows, axis=0).T
    turn_ref[...] = turned.reshape(turn_ref.shape).astype(BF)


def gather_sum(parts):
    ranks, ob, half, cols = parts.shape
    nvir, lanes = cols // ob, 2 * ob * half
    wide = 2 * lanes
    steps = nvir // wide
    return pl.pallas_call(
        gather_sum_kernel,
        grid=(steps,),
        out_shape=[
            jax.ShapeDtypeStruct((ob, ob, half, nvir), F32),
            jax.ShapeDtypeStruct((nvir // half, half, lanes), BF),
        ],
        in_specs=[
            pl.BlockSpec((ranks, ob, half, wide), lambda j: (0, 0, 0, j)),
            pl.BlockSpec((ranks, ob, half, wide), lambda j: (0, 0, 0, j + steps)),
        ],
        out_specs=[
            pl.BlockSpec((ob, ob, half, wide), lambda j: (0, 0, 0, j)),
            pl.BlockSpec((wide // half, half, lanes), lambda j: (j, 0, 0)),
        ],
        compiler_params=vmem(8),
    )(parts, parts)


def density_kernel(e_ref, slot_ref, keep_ref, turn_ref, vc_ref, vall_ref, o_ref):
    ob, _, half, nvir = keep_ref.shape
    ranks, _, lanes = turn_ref.shape
    nv = ranks // 2
    spots = lanes // half
    spot = lax.broadcasted_iota(jnp.int32, (half, lanes), 1) // half
    turned = {}
    for g in range(ranks // spots):
        moved = []
        for j in range(spots):
            x = turn_ref[g * spots + j].astype(F32)
            moved.append([x] + [pltpu.roll(x, n * half, 1) for n in range(1, spots)])
        for ki in range(spots):
            whole = moved[0][(-ki) % spots]
            for j in range(1, spots):
                whole = jnp.where(spot == j, moved[j][(j - ki) % spots], whole)
            turned.setdefault((ki % ob, ki // ob), []).append(whole)
    turned = {ik: jnp.concatenate(x, axis=1) for ik, x in turned.items()}

    def swap(x):
        return pltpu.roll(x, lanes // 2, 1)

    t1, c1, t2, c2 = {}, {}, {}, {}
    for i in range(ob):
        for k in range(ob):
            x1 = keep_ref[i, k]
            x2 = turned[i, k]
            denom = (e_ref[i] + e_ref[ob + k]) - vc_ref[...] - vall_ref[...]
            t1[i, k] = (x1 / denom).astype(BF)
            t2[i, k] = (x2 / denom).astype(BF)
            c1[i, k] = ((2.0 * x1 - x2) / denom).astype(BF)
            c2[i, k] = ((2.0 * x2 - x1) / denom).astype(BF)
    order = [(i, k) for i in range(ob) for k in range(ob)]
    amps = jnp.concatenate([t1[x] for x in order] + [t2[x] for x in order], axis=0)
    contra = jnp.concatenate([c1[x] for x in order] + [c2[x] for x in order], axis=0)
    vt = lax.dot_general(contra, amps, (((0,), (0,)), ((), ())), preferred_element_type=F32)
    split = vt.reshape(nvir // 16, 2, 8, nvir)
    h0 = split[:, 0].reshape(nvir // 2, nvir)
    h1 = split[:, 1].reshape(nvir // 2, nvir)
    low = lax.broadcasted_iota(jnp.int32, (nvir // 2, lanes), 1) < lanes // 2
    planes = (o_ref.shape[1] - 16) // 8
    for j in range(nv // 2):
        x, y = h0[:, j * lanes : (j + 1) * lanes], h1[:, j * lanes : (j + 1) * lanes]
        for n, piece in enumerate((jnp.where(low, x, swap(y)), jnp.where(low, swap(x), y))):
            piece = piece.reshape(2, planes, 2, 8, lanes)
            for slot in range(4):
                rows = piece[slot // 2, :, slot % 2].reshape(8 * planes, lanes)
                o_ref[slot * nv + 2 * j + n, : 8 * planes] = rows.astype(o_ref.dtype)

    def dot(x, y):
        rows = jnp.sum(x.astype(F32) * y.astype(F32), axis=0, keepdims=True)
        return sum(rows[:, j * lanes : (j + 1) * lanes] for j in range(nvir // lanes))

    occ = [-sum(dot(t1[i, k], c1[m, k]) for k in range(ob)) for i in range(ob) for m in range(ob)]
    occ += [-sum(dot(t2[i, k], c2[i, n]) for i in range(ob)) for k in range(ob) for n in range(ob)]
    occ = jnp.concatenate(occ, axis=0)
    stays = lax.broadcasted_iota(jnp.int32, occ.shape, 0) < ob * ob
    goes_to = jnp.where(stays, slot_ref[0], slot_ref[1])
    for slot in range(4):
        mine = jnp.where(goes_to == slot, occ, 0.0)
        high = mine.astype(BF)
        rest = (mine - high.astype(F32)).astype(BF)
        tail = jnp.concatenate([high, rest], axis=0)
        for v in range(nv):
            o_ref[slot * nv + v, 8 * planes :] = tail


def density(energies, slots, keep, turned, vc, vall, planes):
    ranks, _, lanes = turned.shape
    return pl.pallas_call(
        density_kernel,
        out_shape=jax.ShapeDtypeStruct((2 * ranks, 8 * planes + 16, lanes), BF),
        in_specs=[SMEM, SMEM] + [VMEM] * 4,
        out_specs=VMEM,
        compiler_params=vmem(16),
    )(energies, slots, keep, turned, vc, vall)


def plane_sum_kernel(at_ref, p_ref, o_ref):
    total = p_ref[0].astype(F32)
    for src in range(1, p_ref.shape[0]):
        total += p_ref[src].astype(F32)
    planes = o_ref.shape[0]
    n = 8 * planes
    occ = total[n : n + 8] + total[n + 8 : n + 16]
    other = pltpu.roll(occ, 4, 0)
    for z in range(planes):
        o_ref[z, :8] = total[8 * z : 8 * z + 8]
        o_ref[z, 8:] = jnp.where(at_ref[0] == z, occ, 0.0) + jnp.where(at_ref[1] == z, other, 0.0)


def plane_sum(at, parts, planes):
    return pl.pallas_call(
        plane_sum_kernel,
        out_shape=jax.ShapeDtypeStruct((planes, 16, parts.shape[2]), F32),
        in_specs=[SMEM, VMEM],
        out_specs=VMEM,
        compiler_params=vmem(8),
    )(at, parts)


def last_sum_kernel(p_ref, occ_ref, vir_ref):
    total = p_ref[0]
    for src in range(1, p_ref.shape[0]):
        total += p_ref[src]
    slab = vir_ref.shape[1]
    vir_ref[:8] = total[:8, :slab]
    vir_ref[8:] = total[:8, slab:]
    occ = jnp.sum(total[8:], axis=1, keepdims=True)
    ob = occ_ref.shape[0]
    for i in range(ob):
        for m in range(ob):
            occ_ref[i : i + 1, m : m + 1] = occ[ob * i + m : ob * i + m + 1]


def last_sum(parts, ob, slab):
    return pl.pallas_call(
        last_sum_kernel,
        out_shape=[
            jax.ShapeDtypeStruct((ob, ob), F32),
            jax.ShapeDtypeStruct((16, slab), F32),
        ],
        in_specs=[VMEM],
        out_specs=[VMEM, VMEM],
        compiler_params=vmem(4),
    )(parts)


def chip_groups(count, lanes):
    return [
        [(low + core) * lanes + v for v in range(lanes) for core in range(2)]
        for low in range(0, count, 2)
    ]


def plane_groups(count, lanes):
    planes = count // 4
    return [
        [((y * planes + z) * 2 + core) * lanes + v for y in range(2) for core in range(2) for v in range(lanes)]
        for z in range(planes)
    ]


def column_groups(count):
    planes = count // 4
    return [[(y * planes + z) * 2 + core for z in range(planes)] for y in range(2) for core in range(2)]


def by_chip(offset, count, branch, *operands):
    return lax.switch(offset, [functools.partial(branch, m) for m in range(count // 2)], *operands)


def per_device(three_index, occ_energy, vir_energy, partner):
    ob, slab, naux = three_index.shape
    nvir = vir_energy.shape[0]
    count, lanes = lax.axis_size("occ"), lax.axis_size("vir")
    p, v = lax.axis_index("occ"), lax.axis_index("vir")
    offset = jnp.bitwise_xor(p, partner[0])
    chip, core = p // 2, p % 2
    far, cross = offset // 2, offset % 2
    higher = chip > jnp.bitwise_xor(chip, far)
    stay_core = jnp.where(higher, 1 - cross, 0)
    stay = 2 * chip + stay_core
    come = jnp.bitwise_xor(stay, offset)
    half = slab // 2
    groups = chip_groups(count, lanes)

    def over_vir(x):
        return lax.all_to_all(x, "vir", 0, 0, tiled=True)

    def over_chips(x):
        return lax.all_to_all(x, BOTH, 0, 0, axis_index_groups=groups, tiled=True)

    def to_chip(m, x, turn=0):
        route = [
            (a * lanes + w, (a ^ 2 * m) * lanes + (w ^ turn)) for a in range(count) for w in range(lanes)
        ]
        return lax.ppermute(x, BOTH, route) if m else x

    def to_sibling(x):
        return lax.ppermute(x, "occ", [(a, a ^ 1) for a in range(count)])

    row = lanes // 2
    upper = v // row

    def by_half(m):
        return m // (count // 4) == 1 and m % (count // 4) < 2

    def lead_on(m, x):
        if not by_half(m):
            return (to_chip(m, x),)
        stay = lax.dynamic_slice_in_dim(x, upper * row, row)
        turn = lax.dynamic_slice_in_dim(x, (1 - upper) * row, row)
        return to_chip(m, stay), to_chip(m, turn, row)

    def lead_over(m, straight, *turned):
        if not turned:
            return over_vir(straight)
        (turned,) = turned
        flip = upper == 1
        both = jnp.stack(
            [jnp.where(flip, turned, straight), jnp.where(flip, straight, turned)], axis=1
        )
        halves = [list(range(row)), list(range(row, lanes))]
        both = lax.all_to_all(both, "vir", 0, 0, axis_index_groups=halves, tiled=True)
        return jnp.swapaxes(both, 0, 1).reshape((lanes,) + both.shape[2:])

    def exchange(m, at, x, other0, other1, lead):
        def step(run, *operands):
            like = jax.eval_shape(run, *operands)
            never = lambda *_: jax.tree.map(lambda y: jnp.zeros(y.shape, y.dtype), like)
            return lax.cond(partner[0] >= 0, run, never, *operands)

        def spread(*operands):
            mine = over_vir(pick(*operands))
            return mine, mine[:, ob * slab :]

        lead = lead_on(m, lead)
        mine, last = step(spread, at, x, other0, other1)
        if by_half(m):
            lead, last = lax.optimization_barrier((lead, last))
        last = to_chip(m, last)
        lead, mine = lax.optimization_barrier((lead, mine))
        return mine, step(functools.partial(lead_over, m), *lead), last

    lead_rows = slab + slab // 4
    last_rows = ob * slab - lead_rows
    at = jnp.stack([core, (core == stay_core).astype(jnp.int32)])
    their0, their1, lead = cut(at, three_index, lanes, lead_rows)
    other0, other1 = to_sibling(their0), to_sibling(their1)
    lead = jnp.where(core == stay_core, other0, lead)
    mine, come0, come1 = by_chip(far, count, exchange, at, three_index, other0, other1, lead)
    others = to_sibling(product(False, at, mine, come0, come1, ob, slab))
    own = product(True, at, mine, come0, come1, ob, slab)
    keep, turn = gather_sum(over_vir(core_sum(own, others)))
    turned = over_chips(turn)
    energies = jnp.concatenate([
        lax.dynamic_slice_in_dim(occ_energy, stay * ob, ob),
        lax.dynamic_slice_in_dim(occ_energy, come * ob, ob),
    ])
    vc = lax.dynamic_slice_in_dim(vir_energy, v * slab + core * half, half)
    planes = count // 4

    def slot_of(block):
        return block // (2 * planes) * 2 + block % 2

    def plane_of(block):
        return block // 2 % planes

    packed = density(
        energies, jnp.stack([slot_of(stay), slot_of(come)]), keep, turned,
        vc.reshape(half, 1), vir_energy.reshape(1, nvir), planes,
    )
    parts = lax.all_to_all(
        packed, BOTH, 0, 0, axis_index_groups=plane_groups(count, lanes), tiled=True
    )
    pieces = plane_sum(jnp.stack([plane_of(stay), plane_of(come)]), parts, planes)
    parts = lax.all_to_all(
        pieces, "occ", 0, 0, axis_index_groups=column_groups(count), tiled=True
    )
    occ_density, vir_turned = last_sum(parts, ob, slab)
    return occ_density, vir_turned.T


def solution(mesh):
    in_specs = (P("occ", "vir", None), P(), P(), P("occ"))
    out_specs = (P("occ", None), P("vir", "occ"))
    return jax.shard_map(
        per_device, mesh=mesh, in_specs=in_specs, out_specs=out_specs, check_vma=False
    )
```

```python
import functools

import jax
import jax.numpy as jnp
from jax import lax
from jax.experimental import pallas as pl
from jax.experimental.pallas import tpu as pltpu
from jax.sharding import PartitionSpec as P

BF = jnp.bfloat16
F32 = jnp.float32
BOTH = ("occ", "vir")
SMEM = pl.BlockSpec(memory_space=pltpu.SMEM)
VMEM = pl.BlockSpec(memory_space=pltpu.VMEM)
ANY = pl.BlockSpec(memory_space=pl.ANY)
HBM = pl.BlockSpec(memory_space=pltpu.HBM)


def vmem(mib):
    return pltpu.CompilerParams(vmem_limit_bytes=mib * 1024 * 1024)


def copy_all(parts, copies_of, sems):
    def each(w, begin):
        for n, (src, dst) in enumerate(copies_of(w)):
            copy = pltpu.make_async_copy(src, dst, sems.at[w, n])
            copy.start() if begin else copy.wait()

    lax.fori_loop(0, parts, lambda w, _: each(w, True), None)
    lax.fori_loop(0, parts, lambda w, _: each(w, False), None)


def cut_kernel(at_ref, x_ref, their0_ref, their1_ref, own_ref, sems):
    parts, lead, q = own_ref.shape
    slab = x_ref.shape[1]
    more = lead - slab

    def copies_of(w):
        theirs = pl.ds(pl.multiple_of(((1 - at_ref[0]) * parts + w) * q, q), q)
        mine = pl.ds(pl.multiple_of((at_ref[0] * parts + w) * q, q), q)
        copies = [
            (x_ref.at[0, :, theirs], their0_ref.at[w, :slab]),
            (x_ref.at[1, more:, theirs], their1_ref.at[w]),
            (x_ref.at[0, :, mine], own_ref.at[w, :slab]),
        ]
        if more:
            copies += [
                (x_ref.at[1, :more, theirs], their0_ref.at[w, slab:]),
                (x_ref.at[1, :more, mine], own_ref.at[w, slab:]),
            ]
        return copies

    copy_all(parts, copies_of, sems)


def cut(at, x, parts, lead):
    ob, slab, naux = x.shape
    q = naux // (2 * parts)
    return pl.pallas_call(
        cut_kernel,
        out_shape=[
            jax.ShapeDtypeStruct((parts, rows, q), x.dtype)
            for rows in (lead, ob * slab - lead, lead)
        ],
        in_specs=[SMEM, HBM],
        out_specs=[VMEM] * 3,
        scratch_shapes=[pltpu.SemaphoreType.DMA((parts, 5))],
        compiler_params=vmem(8),
    )(at, x)


def pick_kernel(at_ref, x_ref, other0_ref, other1_ref, o_ref, sems):
    parts, rows, q = o_ref.shape
    lead, last = other0_ref.shape[1], other1_ref.shape[1]
    slab = x_ref.shape[1]
    more = lead - slab

    def fill(stays):
        def copies_of(w):
            mine = pl.ds(pl.multiple_of((at_ref[0] * parts + w) * q, q), q)
            if stays:
                return [
                    (x_ref.at[0, :, mine], o_ref.at[w, :slab]),
                    (x_ref.at[1, :, mine], o_ref.at[w, slab : 2 * slab]),
                    (other1_ref.at[w], o_ref.at[w, 2 * slab :]),
                ]
            return [
                (other0_ref.at[w], o_ref.at[w, :lead]),
                (other1_ref.at[w], o_ref.at[w, lead : lead + last]),
                (x_ref.at[1, more:, mine], o_ref.at[w, 2 * slab :]),
            ]

        copy_all(parts, copies_of, sems)

    pl.when(at_ref[1] != 0)(lambda: fill(True))
    pl.when(at_ref[1] == 0)(lambda: fill(False))


def pick(at, x, other0, other1):
    parts, lead, q = other0.shape
    last = other1.shape[1]
    return pl.pallas_call(
        pick_kernel,
        out_shape=jax.ShapeDtypeStruct((parts, lead + 2 * last, q), x.dtype),
        in_specs=[SMEM, HBM, ANY, ANY],
        out_specs=VMEM,
        scratch_shapes=[pltpu.SemaphoreType.DMA((parts, 3))],
        compiler_params=vmem(8),
    )(at, x, other0, other1)


def product_kernel(own, at_ref, mine_ref, come0_ref, come1_ref, o_ref):
    nv, lead, q = come0_ref.shape
    half = o_ref.shape[2]
    slab = 2 * half
    n = nv * slab
    core = at_ref[0] if own else 1 - at_ref[0]
    blocks = [come0_ref[:, :slab], come1_ref[...]]
    if lead > slab:
        blocks[1] = jnp.concatenate([come0_ref[:, slab:], blocks[1]], axis=1)
    start = pl.multiple_of(core * half, half)
    rows = mine_ref[:, pl.ds(start, half)].reshape(nv * half, q)
    for k, block in enumerate(blocks):
        out = lax.dot_general(
            rows, block.reshape(n, q), (((1,), (1,)), ((), ())), preferred_element_type=F32
        )
        o_ref[:, 0, :, k * n : (k + 1) * n] = out.reshape(nv, half, n).astype(o_ref.dtype)


def product(own, at, mine, come0, come1, ob, slab):
    nv, _, q = mine.shape
    cols = ob * nv * slab
    return pl.pallas_call(
        functools.partial(product_kernel, own),
        grid=(ob,),
        out_shape=jax.ShapeDtypeStruct((nv, ob, slab // 2, cols), F32 if own else BF),
        in_specs=[
            SMEM,
            pl.BlockSpec((nv, slab, q), lambda i: (0, i, 0)),
            pl.BlockSpec(come0.shape, lambda i: (0, 0, 0)),
            pl.BlockSpec(come1.shape, lambda i: (0, 0, 0)),
        ],
        out_specs=pl.BlockSpec((nv, 1, slab // 2, cols), lambda i: (0, i, 0, 0)),
        compiler_params=vmem(24),
    )(at, mine, come0, come1)


def core_sum_kernel(own_ref, other_ref, o_ref):
    o_ref[...] = (own_ref[...] + other_ref[...].astype(F32)).astype(BF)


def core_sum(own, other):
    nv, ob, half, cols = own.shape
    spec = pl.BlockSpec((nv, ob, half, cols), lambda r: (r, 0, 0, 0))
    return pl.pallas_call(
        core_sum_kernel,
        grid=(1,),
        out_shape=jax.ShapeDtypeStruct(own.shape, BF),
        in_specs=[spec, spec],
        out_specs=spec,
        compiler_params=vmem(16),
    )(own, other)


def gather_sum_kernel(p0_ref, p1_ref, keep_ref, turn_ref):
    rows = []
    for k, ref in enumerate((p0_ref, p1_ref)):
        total = ref[0].astype(F32)
        for src in range(1, ref.shape[0]):
            total += ref[src].astype(F32)
        keep_ref[:, k] = total
        rows.append(total.reshape(-1, total.shape[2]))
    turned = jnp.concatenate(rows, axis=0).T
    turn_ref[...] = turned.reshape(turn_ref.shape).astype(BF)


def gather_sum(parts):
    ranks, ob, half, cols = parts.shape
    nvir, lanes = cols // ob, 2 * ob * half
    wide = 2 * lanes
    steps = nvir // wide
    return pl.pallas_call(
        gather_sum_kernel,
        grid=(steps,),
        out_shape=[
            jax.ShapeDtypeStruct((ob, ob, half, nvir), F32),
            jax.ShapeDtypeStruct((nvir // half, half, lanes), BF),
        ],
        in_specs=[
            pl.BlockSpec((ranks, ob, half, wide), lambda j: (0, 0, 0, j)),
            pl.BlockSpec((ranks, ob, half, wide), lambda j: (0, 0, 0, j + steps)),
        ],
        out_specs=[
            pl.BlockSpec((ob, ob, half, wide), lambda j: (0, 0, 0, j)),
            pl.BlockSpec((wide // half, half, lanes), lambda j: (j, 0, 0)),
        ],
        compiler_params=vmem(8),
    )(parts, parts)


def density_kernel(e_ref, slot_ref, keep_ref, turn_ref, vc_ref, vall_ref, o_ref):
    ob, _, half, nvir = keep_ref.shape
    ranks, _, lanes = turn_ref.shape
    nv = ranks // 2
    spots = lanes // half
    spot = lax.broadcasted_iota(jnp.int32, (half, lanes), 1) // half
    turned = {}
    for g in range(ranks // spots):
        moved = []
        for j in range(spots):
            x = turn_ref[g * spots + j].astype(F32)
            moved.append([x] + [pltpu.roll(x, n * half, 1) for n in range(1, spots)])
        for ki in range(spots):
            whole = moved[0][(-ki) % spots]
            for j in range(1, spots):
                whole = jnp.where(spot == j, moved[j][(j - ki) % spots], whole)
            turned.setdefault((ki % ob, ki // ob), []).append(whole)
    turned = {ik: jnp.concatenate(x, axis=1) for ik, x in turned.items()}

    def swap(x):
        return pltpu.roll(x, lanes // 2, 1)

    t1, c1, t2, c2 = {}, {}, {}, {}
    for i in range(ob):
        for k in range(ob):
            x1 = keep_ref[i, k]
            x2 = turned[i, k]
            denom = (e_ref[i] + e_ref[ob + k]) - vc_ref[...] - vall_ref[...]
            t1[i, k] = (x1 / denom).astype(BF)
            t2[i, k] = (x2 / denom).astype(BF)
            c1[i, k] = ((2.0 * x1 - x2) / denom).astype(BF)
            c2[i, k] = ((2.0 * x2 - x1) / denom).astype(BF)
    order = [(i, k) for i in range(ob) for k in range(ob)]
    amps = jnp.concatenate([t1[x] for x in order] + [t2[x] for x in order], axis=0)
    contra = jnp.concatenate([c1[x] for x in order] + [c2[x] for x in order], axis=0)
    vt = lax.dot_general(contra, amps, (((0,), (0,)), ((), ())), preferred_element_type=F32)
    split = vt.reshape(nvir // 16, 2, 8, nvir)
    h0 = split[:, 0].reshape(nvir // 2, nvir)
    h1 = split[:, 1].reshape(nvir // 2, nvir)
    low = lax.broadcasted_iota(jnp.int32, (nvir // 2, lanes), 1) < lanes // 2
    planes = (o_ref.shape[1] - 16) // 8
    for j in range(nv // 2):
        x, y = h0[:, j * lanes : (j + 1) * lanes], h1[:, j * lanes : (j + 1) * lanes]
        for n, piece in enumerate((jnp.where(low, x, swap(y)), jnp.where(low, swap(x), y))):
            piece = piece.reshape(2, planes, 2, 8, lanes)
            for slot in range(4):
                rows = piece[slot // 2, :, slot % 2].reshape(8 * planes, lanes)
                o_ref[slot * nv + 2 * j + n, : 8 * planes] = rows.astype(o_ref.dtype)

    def dot(x, y):
        rows = jnp.sum(x.astype(F32) * y.astype(F32), axis=0, keepdims=True)
        return sum(rows[:, j * lanes : (j + 1) * lanes] for j in range(nvir // lanes))

    occ = [-sum(dot(t1[i, k], c1[m, k]) for k in range(ob)) for i in range(ob) for m in range(ob)]
    occ += [-sum(dot(t2[i, k], c2[i, n]) for i in range(ob)) for k in range(ob) for n in range(ob)]
    occ = jnp.concatenate(occ, axis=0)
    stays = lax.broadcasted_iota(jnp.int32, occ.shape, 0) < ob * ob
    goes_to = jnp.where(stays, slot_ref[0], slot_ref[1])
    for slot in range(4):
        mine = jnp.where(goes_to == slot, occ, 0.0)
        high = mine.astype(BF)
        rest = (mine - high.astype(F32)).astype(BF)
        tail = jnp.concatenate([high, rest], axis=0)
        for v in range(nv):
            o_ref[slot * nv + v, 8 * planes :] = tail


def density(energies, slots, keep, turned, vc, vall, planes):
    ranks, _, lanes = turned.shape
    return pl.pallas_call(
        density_kernel,
        out_shape=jax.ShapeDtypeStruct((2 * ranks, 8 * planes + 16, lanes), BF),
        in_specs=[SMEM, SMEM] + [VMEM] * 4,
        out_specs=VMEM,
        compiler_params=vmem(16),
    )(energies, slots, keep, turned, vc, vall)


def plane_sum_kernel(at_ref, p_ref, o_ref):
    total = p_ref[0].astype(F32)
    for src in range(1, p_ref.shape[0]):
        total += p_ref[src].astype(F32)
    planes = o_ref.shape[0]
    n = 8 * planes
    occ = total[n : n + 8] + total[n + 8 : n + 16]
    other = pltpu.roll(occ, 4, 0)
    for z in range(planes):
        o_ref[z, :8] = total[8 * z : 8 * z + 8]
        o_ref[z, 8:] = jnp.where(at_ref[0] == z, occ, 0.0) + jnp.where(at_ref[1] == z, other, 0.0)


def plane_sum(at, parts, planes):
    return pl.pallas_call(
        plane_sum_kernel,
        out_shape=jax.ShapeDtypeStruct((planes, 16, parts.shape[2]), F32),
        in_specs=[SMEM, VMEM],
        out_specs=VMEM,
        compiler_params=vmem(8),
    )(at, parts)


def last_sum_kernel(p_ref, occ_ref, vir_ref):
    total = p_ref[0]
    for src in range(1, p_ref.shape[0]):
        total += p_ref[src]
    slab = vir_ref.shape[1]
    vir_ref[:8] = total[:8, :slab]
    vir_ref[8:] = total[:8, slab:]
    occ = jnp.sum(total[8:], axis=1, keepdims=True)
    ob = occ_ref.shape[0]
    for i in range(ob):
        for m in range(ob):
            occ_ref[i : i + 1, m : m + 1] = occ[ob * i + m : ob * i + m + 1]


def last_sum(parts, ob, slab):
    return pl.pallas_call(
        last_sum_kernel,
        out_shape=[
            jax.ShapeDtypeStruct((ob, ob), F32),
            jax.ShapeDtypeStruct((16, slab), F32),
        ],
        in_specs=[VMEM],
        out_specs=[VMEM, VMEM],
        compiler_params=vmem(4),
    )(parts)


def chip_groups(count, lanes):
    return [
        [(low + core) * lanes + v for v in range(lanes) for core in range(2)]
        for low in range(0, count, 2)
    ]


def plane_groups(count, lanes):
    planes = count // 4
    return [
        [((y * planes + z) * 2 + core) * lanes + v for y in range(2) for core in range(2) for v in range(lanes)]
        for z in range(planes)
    ]


def column_groups(count):
    planes = count // 4
    return [[(y * planes + z) * 2 + core for z in range(planes)] for y in range(2) for core in range(2)]


def by_chip(offset, count, branch, *operands):
    return lax.switch(offset, [functools.partial(branch, m) for m in range(count // 2)], *operands)


def per_device(three_index, occ_energy, vir_energy, partner):
    ob, slab, naux = three_index.shape
    nvir = vir_energy.shape[0]
    count, lanes = lax.axis_size("occ"), lax.axis_size("vir")
    p, v = lax.axis_index("occ"), lax.axis_index("vir")
    offset = jnp.bitwise_xor(p, partner[0])
    chip, core = p // 2, p % 2
    far, cross = offset // 2, offset % 2
    higher = chip > jnp.bitwise_xor(chip, far)
    stay_core = jnp.where(higher, 1 - cross, 0)
    stay = 2 * chip + stay_core
    come = jnp.bitwise_xor(stay, offset)
    half = slab // 2
    groups = chip_groups(count, lanes)

    def over_vir(x):
        return lax.all_to_all(x, "vir", 0, 0, tiled=True)

    def over_chips(x):
        return lax.all_to_all(x, BOTH, 0, 0, axis_index_groups=groups, tiled=True)

    def to_chip(m, x, turn=0):
        route = [
            (a * lanes + w, (a ^ 2 * m) * lanes + (w ^ turn)) for a in range(count) for w in range(lanes)
        ]
        return lax.ppermute(x, BOTH, route) if m else x

    def to_sibling(x):
        return lax.ppermute(x, "occ", [(a, a ^ 1) for a in range(count)])

    row = lanes // 2
    upper = v // row

    def by_half(m):
        return m // (count // 4) == 1 and m % (count // 4) < 2

    def lead_on(m, x):
        if not by_half(m):
            return (to_chip(m, x),)
        stay = lax.dynamic_slice_in_dim(x, upper * row, row)
        turn = lax.dynamic_slice_in_dim(x, (1 - upper) * row, row)
        return to_chip(m, stay), to_chip(m, turn, row)

    def lead_over(m, straight, *turned):
        if not turned:
            return over_vir(straight)
        (turned,) = turned
        flip = upper == 1
        both = jnp.stack(
            [jnp.where(flip, turned, straight), jnp.where(flip, straight, turned)], axis=1
        )
        halves = [list(range(row)), list(range(row, lanes))]
        both = lax.all_to_all(both, "vir", 0, 0, axis_index_groups=halves, tiled=True)
        return jnp.swapaxes(both, 0, 1).reshape((lanes,) + both.shape[2:])

    def exchange(m, at, x, other0, other1, lead):
        def step(run, *operands):
            like = jax.eval_shape(run, *operands)
            never = lambda *_: jax.tree.map(lambda y: jnp.zeros(y.shape, y.dtype), like)
            return lax.cond(partner[0] >= 0, run, never, *operands)

        def spread(*operands):
            mine = over_vir(pick(*operands))
            return mine, mine[:, ob * slab :]

        lead = lead_on(m, lead)
        mine, last = step(spread, at, x, other0, other1)
        if by_half(m):
            lead, last = lax.optimization_barrier((lead, last))
        last = to_chip(m, last)
        lead, mine = lax.optimization_barrier((lead, mine))
        return mine, step(functools.partial(lead_over, m), *lead), last

    lead_rows = slab + slab // 4
    last_rows = ob * slab - lead_rows
    at = jnp.stack([core, (core == stay_core).astype(jnp.int32)])
    their0, their1, lead = cut(at, three_index, lanes, lead_rows)
    other0, other1 = to_sibling(their0), to_sibling(their1)
    lead = jnp.where(core == stay_core, other0, lead)
    mine, come0, come1 = by_chip(far, count, exchange, at, three_index, other0, other1, lead)
    others = to_sibling(product(False, at, mine, come0, come1, ob, slab))
    own = product(True, at, mine, come0, come1, ob, slab)
    keep, turn = gather_sum(over_vir(core_sum(own, others)))
    turned = over_chips(turn)
    energies = jnp.concatenate([
        lax.dynamic_slice_in_dim(occ_energy, stay * ob, ob),
        lax.dynamic_slice_in_dim(occ_energy, come * ob, ob),
    ])
    vc = lax.dynamic_slice_in_dim(vir_energy, v * slab + core * half, half)
    planes = count // 4

    def slot_of(block):
        return block // (2 * planes) * 2 + block % 2

    def plane_of(block):
        return block // 2 % planes

    packed = density(
        energies, jnp.stack([slot_of(stay), slot_of(come)]), keep, turned,
        vc.reshape(half, 1), vir_energy.reshape(1, nvir), planes,
    )
    parts = lax.all_to_all(
        packed, BOTH, 0, 0, axis_index_groups=plane_groups(count, lanes), tiled=True
    )
    pieces = plane_sum(jnp.stack([plane_of(stay), plane_of(come)]), parts, planes)
    parts = lax.all_to_all(
        pieces, "occ", 0, 0, axis_index_groups=column_groups(count), tiled=True
    )
    occ_density, vir_turned = last_sum(parts, ob, slab)
    return occ_density, vir_turned.T


def solution(mesh):
    in_specs = (P("occ", "vir", None), P(), P(), P("occ"))
    out_specs = (P("occ", None), P("vir", "occ"))
    return jax.shard_map(
        per_device, mesh=mesh, in_specs=in_specs, out_specs=out_specs, check_vma=False
    )
```
